128 devices in a mesh: batch: 16 (over z, y), tensor: 8 (over x, core).
Axes of the slice: x: 4, y: 4, z: 4, core: 2. Of those that a mesh axis runs over, the one named last changes fastest.
Arguments:
- x_new: bfloat16 [256, 8192], P('batch', 'tensor'), may hold values from -6 to 6
- z_gate: bfloat16 [256, 8192], P('batch', 'tensor'), may hold values from -6 to 6
- bc_new: bfloat16 [256, 2048], P('batch'), may hold values from -6 to 6
- dt_raw: float32 [256, 128], P('batch', 'tensor'), may hold values from -4 to 4
- conv_x: bfloat16 [256, 3, 8192], P('batch', None, 'tensor'), may hold values from -6 to 6
- conv_bc: bfloat16 [256, 3, 2048], P('batch'), may hold values from -6 to 6
- conv_x_weight: float32 [4, 8192], P(None, 'tensor'), may hold values from -3 to 3
- conv_bc_weight: float32 [4, 2048], replicated, may hold values from -3 to 3
- dt_bias: float32 [128], P('tensor'), may hold values from -5 to -1
- a_log: float32 [128], P('tensor'), may hold values from 0 to 3
- d_skip: float32 [128], P('tensor'), may hold values from 0.5 to 1.5
- ssm_state: bfloat16 [256, 128, 64, 256], P('batch', 'tensor'), may hold values from -0.59765625 to 0.59765625
- norm_gain: float32 [8192], P('tensor'), may hold values from 0.5 to 1.5
- out_weight: bfloat16 [8192, 8192], P('tensor', 'batch'), may hold values from -0.0625 to 0.0625
- residual: bfloat16 [256, 8192], P('tensor', 'batch'), may hold values from -6 to 6
- final_gain: float32 [8192], P('batch'), may hold values from 0.5 to 1.5
- vocab_weight: bfloat16 [65536, 8192], P(('batch', 'tensor')), may hold values from -0.1875 to 0.1875
- tile_ids: int32 [256, 4], replicated, may hold values from 0 to 511, as said below
- tile_valid: int32 [256, 4], replicated, may hold values from 0 to 1
- sampled: int32 [256], replicated, may hold values from 0 to 65535, as said below
Outputs:
- new_state: bfloat16 [256, 128, 64, 256], P('batch', 'tensor')
- layer_out: bfloat16 [256, 8192], P('tensor', 'batch')
- token_logprob: float32 [256], P(('batch', 'tensor'))
The draws below stay inside these ranges and needn't reach their ends.
Inputs may be any that keep to these rules, and one draw needn't show every extreme that they name: `tile_ids`: A row's 4 tile ids are distinct; tile t holds the entries t * 128 to t * 128 + 127 and belongs to vocabulary shard t // 4; a row's tiles lie in two shards. In each aligned block of 32 rows, at most 1 row has used tiles in any one shard, and some shard is used by exactly 1 row of a block. Each row's sampled token lies in the tile of one of its used slots.
All inputs are finite; a program needn't handle non-finite values.
Results may differ from the reference program's by a relative error of at most 0.0041.
Values may be sent and summed in bfloat16 or wider, within the bound.
No kernel may reach another device: no remote copies, remote signals or barrier semaphores. Data moves between devices by JAX's collectives and lax.ppermute only.
A program may use at most 128 MiB of HBM per device.

```python
import jax
import jax.numpy as jnp
from jax import lax

D = 8192
HEAD_DIM = 64
STATE = 256
GROUP_HEADS = 32
CONV = 4
TILE = 128
TILES_DEV = 4
SLOTS = 4
HEADS = 128
GROUPS = 4
INNER = 8192
ROWS = 256
VOCAB = 65536
BLOCK_ROWS = 32
CAP = 1


def tile_table(key):
    tile_count = VOCAB // TILE
    shard_count = tile_count // TILES_DEV
    block_count = ROWS // BLOCK_ROWS
    key_perm, key_first, key_second, key_noise, key_valid, key_slot, key_offset = jax.random.split(key, 7)
    perm_keys = jax.random.split(key_perm, block_count)
    perms = jax.vmap(lambda one_key: jax.random.permutation(one_key, shard_count))(perm_keys).astype(jnp.int32)
    block_index = jnp.arange(block_count, dtype=jnp.int32)
    target = jnp.where(block_index == 0, shard_count - 1, jnp.where(block_index == 1, 0, perms[:, 0])).astype(jnp.int32)
    position = jnp.argmax((perms == target[:, None]).astype(jnp.int32), axis=1).astype(jnp.int32)
    shard_index = jnp.arange(shard_count, dtype=jnp.int32)
    leading = perms[:, :1]
    perms = jnp.where(shard_index[None, :] == 0, target[:, None], jnp.where(shard_index[None, :] == position[:, None], leading, perms)).astype(jnp.int32)
    repeated = jnp.tile(perms, (1, CAP))[:, :2 * BLOCK_ROWS]
    pairs = repeated.reshape(ROWS, 2)
    shard_first = pairs[:, 0]
    shard_second = pairs[:, 1]
    row_index = jnp.arange(ROWS, dtype=jnp.int32)
    offset_first = jax.random.randint(key_first, (ROWS,), 0, TILES_DEV).astype(jnp.int32)
    offset_first = jnp.where(row_index == 0, TILES_DEV - 1, jnp.where(row_index == BLOCK_ROWS, 0, offset_first))
    offset_second = jax.random.randint(key_second, (ROWS,), 0, TILES_DEV).astype(jnp.int32)
    local = jnp.arange(TILES_DEV, dtype=jnp.int32)
    candidates = jnp.concatenate([shard_first[:, None] * TILES_DEV + local[None, :], shard_second[:, None] * TILES_DEV + local[None, :]], axis=1)
    cand_index = jnp.arange(2 * TILES_DEV, dtype=jnp.int32)
    noise_draw = jax.random.randint(key_noise, (ROWS, 2 * TILES_DEV), 0, 1024)
    boost_value = 1024 * 2 * TILES_DEV
    scores = noise_draw * (2 * TILES_DEV) + cand_index[None, :]
    scores = scores + 2 * boost_value * (cand_index[None, :] == offset_first[:, None]).astype(jnp.int32)
    scores = scores + boost_value * (cand_index[None, :] == TILES_DEV + offset_second[:, None]).astype(jnp.int32)
    unused, order = lax.top_k(scores, SLOTS)
    slot_tiles = jnp.take_along_axis(candidates, order.astype(jnp.int32), axis=1).astype(jnp.int32)
    slot_valid = jax.random.randint(key_valid, (ROWS, SLOTS), 0, 2).astype(jnp.int32)
    chosen_slot = jax.random.randint(key_slot, (ROWS,), 0, SLOTS).astype(jnp.int32)
    chosen_slot = jnp.where((row_index == 0) | (row_index == BLOCK_ROWS), 0, chosen_slot)
    slot_index = jnp.arange(SLOTS, dtype=jnp.int32)
    slot_valid = jnp.where((slot_index[None, :] == chosen_slot[:, None]) | (slot_index[None, :] == 0), 1, slot_valid).astype(jnp.int32)
    offset = jax.random.randint(key_offset, (ROWS,), 0, TILE).astype(jnp.int32)
    offset = jnp.where(row_index == 0, TILE - 1, jnp.where(row_index == BLOCK_ROWS, 0, offset))
    chosen_tile = jnp.take_along_axis(slot_tiles, chosen_slot[:, None], axis=1)[:, 0]
    sampled_draw = (chosen_tile * TILE + offset).astype(jnp.int32)
    return (slot_tiles, slot_valid, sampled_draw)


def draw_tile_ids(key, part):
    return tile_table(key)[0]


def draw_tile_valid(key, part):
    return tile_table(key)[1]


def draw_sampled(key, part):
    return tile_table(key)[2]


def levels(key, extent, shards, least, largest):
    level, own = 1.0, jax.random.fold_in(key, 6)
    for dim, parts in shards:
        steps = jnp.exp(jax.random.uniform(jax.random.fold_in(own, dim), (parts,), jnp.float32, least / len(shards), largest / len(shards)))
        level = level * jnp.repeat(steps, extent[dim] // parts).reshape([-1 if axis == dim else 1 for axis in range(len(extent))])
    return level


def noise(stream_key, shape, deviation, reach, shards=(), held_as=jnp.bfloat16):
    array = deviation * jax.random.normal(stream_key, shape, jnp.float32)
    if shards:
        array = array * levels(stream_key, shape, shards, -0.22, 0.18)
    return jnp.clip(array, -reach, reach).astype(held_as)


def setup_inputs(seed: int = 0) -> dict:
    keys = jax.random.split(jax.random.key(seed), 21)
    return {
        "x_new": noise(keys[0], (ROWS, INNER), 1.0, 6.0, ((0, 16), (1, 8))),
        "z_gate": noise(keys[1], (ROWS, INNER), 1.0, 6.0, ((0, 16), (1, 8))),
        "bc_new": noise(keys[2], (ROWS, 2 * GROUPS * STATE), 1.0, 6.0, ((0, 16),)),
        "dt_raw": noise(keys[3], (ROWS, HEADS), 1.0, 4.0, ((0, 16), (1, 8)), jnp.float32),
        "conv_x": noise(keys[4], (ROWS, CONV - 1, INNER), 1.0, 6.0, ((0, 16), (2, 8))),
        "conv_bc": noise(keys[5], (ROWS, CONV - 1, 2 * GROUPS * STATE), 1.0, 6.0, ((0, 16),)),
        "conv_x_weight": noise(keys[6], (CONV, INNER), 0.5, 3.0, ((1, 8),), jnp.float32),
        "conv_bc_weight": noise(keys[7], (CONV, 2 * GROUPS * STATE), 0.5, 3.0, (), jnp.float32),
        "dt_bias": jnp.clip(-5.0 + 4.0 * jax.random.uniform(keys[8], (HEADS,), jnp.float32) ** levels(keys[8], (HEADS,), ((0, 8),), -0.2, 0.2), -5.0, -1.0),
        "a_log": jnp.clip(3.0 * jax.random.uniform(keys[9], (HEADS,), jnp.float32) ** levels(keys[9], (HEADS,), ((0, 8),), -0.2, 0.2), 0.0, 3.0),
        "d_skip": jnp.clip(0.5 + 1.0 * jax.random.uniform(keys[10], (HEADS,), jnp.float32) ** levels(keys[10], (HEADS,), ((0, 8),), -0.2, 0.2), 0.5, 1.5),
        "ssm_state": noise(keys[11], (ROWS, HEADS, HEAD_DIM, STATE), 0.1, 0.59765625, ((0, 16), (1, 8))),
        "norm_gain": jnp.clip(1.0 + 0.1 * jax.random.normal(keys[12], (INNER,), jnp.float32), 0.5, 1.5),
        "out_weight": noise(keys[13], (INNER, D), INNER ** -0.5, 0.0625, ((0, 8), (1, 16))),
        "residual": noise(keys[14], (ROWS, D), 1.0, 6.0, ((0, 8), (1, 16))),
        "final_gain": jnp.clip(1.0 + 0.1 * jax.random.normal(keys[15], (D,), jnp.float32), 0.5, 1.5),
        "vocab_weight": noise(keys[16], (VOCAB, D), (D // 9) ** -0.5, 0.1875, ((0, 128),)),
        "tile_ids": draw_tile_ids(jax.random.fold_in(keys[20], 71), 0),
        "tile_valid": draw_tile_valid(jax.random.fold_in(keys[20], 71), 0),
        "sampled": draw_sampled(jax.random.fold_in(keys[20], 71), 0),
    }


epsilon = 1e-05

def conv_step(window, newest, weight):
    accum = lax.optimization_barrier(jnp.sum(window.astype(jnp.float32) * weight[None, :-1, :], axis=1))
    accum = accum + newest.astype(jnp.float32) * weight[-1][None, :]
    return jax.nn.silu(accum)

def one_row(packed):
    state_row, decay_row, step_row, value_row, input_row, output_row = packed
    state_full = decay_row[:, None, None] * state_row.astype(jnp.float32)
    state_full = state_full + (step_row[:, None] * value_row)[:, :, None] * input_row[:, None, :]
    ssm_row = jnp.einsum('hpn,hn->hp', state_full, output_row, precision=lax.Precision.HIGHEST)
    return (state_full.astype(jnp.bfloat16), ssm_row)

def reference(x_new, z_gate, bc_new, dt_raw, conv_x, conv_bc, conv_x_weight, conv_bc_weight, dt_bias, a_log, d_skip, ssm_state, norm_gain, out_weight, residual, final_gain, vocab_weight, tile_ids, tile_valid, sampled):
    conv_out = conv_step(conv_x, x_new, conv_x_weight)
    bc_conv = conv_step(conv_bc, bc_new, conv_bc_weight)
    b_in = bc_conv[:, :GROUPS * STATE].reshape(ROWS, GROUPS, STATE)
    c_out = bc_conv[:, GROUPS * STATE:].reshape(ROWS, GROUPS, STATE)
    b_heads = jnp.repeat(b_in, GROUP_HEADS, axis=1)
    c_heads = jnp.repeat(c_out, GROUP_HEADS, axis=1)
    step_size = jax.nn.softplus(dt_raw + dt_bias[None, :])
    decay_rate = jnp.exp(-jnp.exp(a_log)[None, :] * step_size)
    x_heads = conv_out.reshape(ROWS, HEADS, HEAD_DIM)
    new_state, ssm_out = lax.map(one_row, (ssm_state, decay_rate, step_size, x_heads, b_heads, c_heads))
    ssm_out = ssm_out + d_skip[None, :, None] * x_heads
    gated = ssm_out.reshape(ROWS, INNER) * jax.nn.silu(z_gate.astype(jnp.float32))
    grouped = gated.reshape(ROWS, GROUPS, GROUP_HEADS * HEAD_DIM)
    mean_sq = lax.optimization_barrier(jnp.mean(grouped * grouped, axis=-1, keepdims=True))
    normed = ((grouped * lax.rsqrt(mean_sq + epsilon)).reshape(ROWS, INNER) * norm_gain[None, :]).astype(jnp.bfloat16)
    mixed = jnp.dot(normed, out_weight, preferred_element_type=jnp.float32)
    layer_out = (residual.astype(jnp.float32) + mixed).astype(jnp.bfloat16)
    layer_float = layer_out.astype(jnp.float32)
    row_sq = lax.optimization_barrier(jnp.mean(layer_float * layer_float, axis=-1, keepdims=True))
    final = (layer_float * lax.rsqrt(row_sq + epsilon) * final_gain[None, :]).astype(jnp.bfloat16)
    logits = jnp.dot(final, vocab_weight.T, preferred_element_type=jnp.float32)
    tile_count = VOCAB // TILE
    tile_index = jnp.arange(tile_count, dtype=jnp.int32)
    hits = (tile_ids[:, :, None] == tile_index[None, None, :]).astype(jnp.float32) * tile_valid[:, :, None].astype(jnp.float32)
    tile_mask = jnp.where(lax.optimization_barrier(jnp.sum(hits, axis=1)) > 0.5, 1.0, 0.0).astype(jnp.float32)
    masked_exp = jnp.exp(logits).reshape(ROWS, tile_count, TILE) * tile_mask[:, :, None]
    totals = lax.optimization_barrier(jnp.sum(masked_exp, axis=(1, 2)))
    picked = jnp.take_along_axis(logits, sampled[:, None].astype(jnp.int32), axis=1)[:, 0]
    token_logprob = picked - jnp.log(totals)
    return (new_state, layer_out, token_logprob)
```

```python
import functools

import jax
import jax.numpy as jnp
from jax import lax
from jax.experimental import pallas as pl
from jax.experimental.pallas import tpu as pltpu
from jax.sharding import PartitionSpec as P

D = 8192
HEAD_DIM = 64
STATE = 256
GROUP_HEADS = 32
GROUPS = 4
TILE = 128
TILES_DEV = 4
BLOCK_ROWS = 32

ROWS = 16
CHAN = 1024
HEADS = 16
KB = CHAN // 128
LINES = KB * ROWS
COLS = 512
BATCH = 16
TENSOR = 8
DEVICES = BATCH * TENSOR
SHARD = TILES_DEV * TILE

epsilon = 1e-05
f32 = jnp.float32
bf16 = jnp.bfloat16
HBM = pl.BlockSpec(memory_space=pltpu.HBM)
VMEM = pl.BlockSpec(memory_space=pltpu.VMEM)
HIGHEST = lax.Precision.HIGHEST


def split(value, parts):
    pieces = []
    for _ in range(parts):
        piece = value.astype(bf16)
        pieces.append(piece)
        value = value - piece.astype(f32)
    return pieces


def silu(value):
    return value / (1.0 + jnp.exp(-value))


def dot(a, b, contract=((1,), (0,)), precision=None):
    return lax.dot_general(a, b, (contract, ((), ())), precision=precision, preferred_element_type=f32)


def iota(shape, dim):
    return lax.broadcasted_iota(jnp.int32, shape, dim)


def tables_kernel(tab, sel, mask, pick, place):
    tensor = lax.axis_index("tensor")
    shard = lax.axis_index("batch") * TENSOR + tensor
    own = tab[pl.ds(pl.multiple_of(tensor * BLOCK_ROWS, BLOCK_ROWS), BLOCK_ROWS), :]
    lanes = iota((BLOCK_ROWS, DEVICES), 1)
    used = jnp.zeros((BLOCK_ROWS, DEVICES), f32)
    for slot in range(4):
        tiles = own[:, slot : slot + 1]
        valid = own[:, 4 + slot : 5 + slot]
        hit = jnp.where(valid == 1, tiles >> 2, -1) == lanes
        used = jnp.where(hit, 1.0, used)
    sel[...] = used
    rows = DEVICES * 2
    whole = tab[...]
    tile = shard * TILES_DEV + iota((rows, SHARD), 1) // TILE
    held = jnp.zeros((rows, SHARD), f32)
    mine = jnp.zeros((rows, 1), f32)
    for slot in range(4):
        tiles = jnp.where(whole[:, 4 + slot : 5 + slot] == 1, whole[:, slot : slot + 1], -1)
        held = jnp.where(tiles == tile, 1.0, held)
        mine = jnp.where((tiles >> 2) == shard, 1.0, mine)
    chosen = jnp.where(whole[:, 8:9] == shard * SHARD + iota((rows, SHARD), 1), 1.0, 0.0)
    block = jnp.where(iota((8, rows), 1) // BLOCK_ROWS == iota((8, rows), 0), 1.0, 0.0).astype(bf16)
    mask[...] = dot(block, held.astype(bf16))
    pick[...] = dot(block, chosen.astype(bf16))
    lane = iota((rows, 128), 1)
    parity = (lane % 2 == iota((rows, 128), 0) % 2) & (lane < 4)
    spread = jnp.where(parity, mine, 0.0).astype(bf16)
    home = jnp.where(iota((DEVICES, rows), 1) // 2 == iota((DEVICES, rows), 0), 1.0, 0.0).astype(bf16)
    place[...] = dot(home, spread)


def ssm_kernel(
    x_new, z_gate, bc_new, dt_raw, conv_x, conv_bc, wx, wbc, dt_bias, a_log, d_skip, state, gain, final_gain,
    new_state, sent,
    x_v, z_v, b_v, c_v, dt_v, cx_v, cb_v, cc_v, wx_v, wb_v, wc_v, bias_v, alog_v, skip_v, gain_v, fg_v,
    state_v, out_v, acc, decay_v, sx_t, b_pieces, c_pieces, small_sem, in_sem, out_sem,
):
    group = lax.axis_index("tensor") // 2
    first = pl.ds(pl.multiple_of(group * STATE, STATE), STATE)
    second = pl.ds(pl.multiple_of((GROUPS + group) * STATE, STATE), STATE)
    pairs = [
        (dt_raw, dt_v), (dt_bias, bias_v), (a_log, alog_v), (d_skip, skip_v),
        (conv_x, cx_v), (x_new, x_v), (wx, wx_v),
        (conv_bc.at[:, :, first], cb_v), (conv_bc.at[:, :, second], cc_v),
        (bc_new.at[:, first], b_v), (bc_new.at[:, second], c_v),
        (wbc.at[:, first], wb_v), (wbc.at[:, second], wc_v),
        (z_gate, z_v), (gain, gain_v), (final_gain, fg_v),
    ]
    copies = [pltpu.make_async_copy(src, dst, small_sem.at[n]) for n, (src, dst) in enumerate(pairs)]
    for copy in copies:
        copy.start()

    def row_in(r):
        return pltpu.make_async_copy(state.at[r], state_v.at[r], in_sem.at[r])

    def row_out(r):
        return pltpu.make_async_copy(out_v.at[r], new_state.at[r], out_sem.at[r])

    for r in range(ROWS):
        row_in(r).start()
    for copy in copies:
        copy.wait()

    def conv(window, newest, weight):
        total = newest[...].astype(f32) * weight[3:4, :]
        for k in range(3):
            total = total + window[k].astype(f32) * weight[k : k + 1, :]
        return silu(total)

    raw = dt_v[...] + bias_v[...]
    step = jnp.maximum(raw, 0.0) + jnp.log1p(jnp.exp(-jnp.abs(raw)))
    decay = jnp.exp(-jnp.exp(alog_v[...]) * step)
    decay_v[...] = decay
    spread = jnp.where(iota((HEADS, CHAN), 1) // HEAD_DIM == iota((HEADS, CHAN), 0), 1.0, 0.0)
    wide = dot(jnp.concatenate([step, decay, jnp.broadcast_to(skip_v[...], (8, HEADS))], 0), spread, precision=HIGHEST)
    step_c, decay_c, skip_c = wide[:ROWS], wide[ROWS : 2 * ROWS], wide[2 * ROWS : 2 * ROWS + 1]
    conv_out = conv(cx_v, x_v, wx_v)
    b_in = conv(cb_v, b_v, wb_v)
    c_out = conv(cc_v, c_v, wc_v)
    sx = step_c * conv_out
    sx_hi, sx_lo = split(sx, 2)
    sx_t[...] = jnp.concatenate([sx_hi.astype(f32), sx_lo.astype(f32), sx_hi.astype(f32)], 0).T.astype(bf16)
    b_hi, b_lo = split(b_in, 2)
    b_pieces[...] = jnp.concatenate([b_hi.astype(f32), b_hi.astype(f32), b_lo.astype(f32)], 0)
    c_pieces[...] = jnp.concatenate([piece.astype(f32) for piece in split(c_out, 3)], 0)
    acc[...] = jnp.zeros_like(acc)

    def one_row(r, carry):
        row_in(r).wait()
        on_row = iota((3 * ROWS, STATE), 0) % ROWS == r
        c_row = jnp.where(on_row, c_pieces[...], 0.0).astype(bf16)
        b_row = jnp.where(on_row, b_pieces[...], 0.0).astype(bf16)
        scale = decay_v[pl.ds(r, 1), :]
        for n in range(4):
            part = slice(n * 256, (n + 1) * 256)
            held = state_v[r, part, :]
            got = dot(c_row, held, ((1,), (1,)))
            acc[:, part] += got[:ROWS] + got[ROWS : 2 * ROWS] + got[2 * ROWS :]
        for n in range(8):
            part = slice(n * 128, (n + 1) * 128)
            outer = dot(sx_t[part, :], b_row)
            for m in range(2):
                head = 2 * n + m
                rows = slice(head * HEAD_DIM, (head + 1) * HEAD_DIM)
                fresh = scale[:, head : head + 1] * state_v[r, rows, :].astype(f32)
                out_v[r, rows, :] = (fresh + outer[m * HEAD_DIM : (m + 1) * HEAD_DIM]).astype(bf16)
        row_out(r).start()
        return carry

    lax.fori_loop(0, ROWS, one_row, 0)
    inner = jnp.sum(b_in * c_out, axis=1, keepdims=True)
    ssm_out = decay_c * acc[...] + sx * inner + skip_c * conv_out
    gated = ssm_out * silu(z_v[...].astype(f32))
    scaled = (gated * gain_v[...]).astype(bf16)
    hi, mid, lo = [piece.astype(f32) for piece in split(fg_v[...], 3)]
    tail = jnp.concatenate([hi, mid, lo, jnp.zeros_like(hi)], 0).astype(bf16)
    for b in range(BATCH):
        for k in range(KB):
            sent[b, k * ROWS : (k + 1) * ROWS, :] = scaled[:, k * 128 : (k + 1) * 128]
        sent[b, LINES : LINES + 16, :] = tail

    def finish(r, carry):
        row_out(r).wait()
        return carry

    lax.fori_loop(0, ROWS, finish, 0)


def project_kernel(got, weight, gain, sent, final_gain, lhs):
    for b in range(BATCH):
        for k in range(KB):
            lhs[b * ROWS : (b + 1) * ROWS, k * 128 : (k + 1) * 128] = got[b, k * ROWS : (k + 1) * ROWS, :]
        pieces = got[b, LINES : LINES + 16, :].astype(f32)
        final_gain[b * 4 : b * 4 + 4, :] = pieces[0:4] + pieces[4:8] + pieces[8:12]
    inverse = 1.0 / gain[...]
    inverse = inverse * inverse
    lane = iota((128, 128), 1)
    for n in range(2):
        rows = lhs[n * 128 : (n + 1) * 128, :]
        product = dot(rows, weight[...])
        wide = rows.astype(f32)
        square = jnp.sum(wide * wide * inverse, axis=1, keepdims=True)
        hi, mid, lo = [piece.astype(f32) for piece in split(square, 3)]
        tail = jnp.where(lane == 0, hi, jnp.where(lane == 1, mid, jnp.where(lane == 2, lo, 0.0)))
        for m in range(4):
            part = slice(m * BLOCK_ROWS, (m + 1) * BLOCK_ROWS)
            sent[n * 4 + m, :, :COLS] = product[part].astype(bf16)
            sent[n * 4 + m, :, COLS:] = tail[part].astype(bf16)


def layer_kernel(got, residual, sel, layer_out, sent, lines):
    mixed = jnp.zeros((BLOCK_ROWS, COLS), f32)
    for g in range(GROUPS):
        both = got[2 * g].astype(f32) + got[2 * g + 1].astype(f32)
        square = jnp.sum(both[:, COLS:], axis=1, keepdims=True)
        mixed = mixed + both[:, :COLS] * lax.rsqrt(square / (GROUP_HEADS * HEAD_DIM) + epsilon)
    layer = (residual[...].astype(f32) + mixed).astype(bf16)
    layer_out[...] = layer
    pick = sel[...].astype(bf16)
    for q in range(4):
        rows = dot(pick, layer[:, q * 128 : (q + 1) * 128], ((0,), (0,)))
        lines[pl.ds(q, DEVICES, stride=4), :] = rows
    sent[...] = lines[...].astype(bf16)


def logits_kernel(got, gain, mask, pick, place, vocab, sent, lines, lhs, vocab_v, sem):
    parts = 8
    width = D // parts

    def chunk(n):
        part = pl.ds(n * width, width)
        return pltpu.make_async_copy(vocab.at[:, part], vocab_v.at[:, part], sem.at[n])

    for n in range(parts):
        chunk(n).start()
    lines[...] = got[...].astype(f32)
    square = jnp.zeros((8, 128), f32)
    for b in range(BATCH):
        for q in range(4):
            value = lines[pl.ds(b * 32 + q, 8, stride=4), :]
            square = square + value * value
    scale = lax.rsqrt(jnp.sum(square, axis=1, keepdims=True) / D + epsilon)
    for b in range(BATCH):
        for q in range(4):
            n = b * 4 + q
            value = lines[pl.ds(b * 32 + q, 8, stride=4), :] * scale * gain[n : n + 1, :]
            lhs[:, n * 128 : (n + 1) * 128] = jnp.concatenate([value, jnp.zeros_like(value)], 0).astype(bf16)
    logits = jnp.zeros((16, SHARD), f32)
    for n in range(parts):
        chunk(n).wait()
        part = slice(n * width, (n + 1) * width)
        logits = logits + dot(lhs[:, part], vocab_v[:, part], ((1,), (1,)))
    logits = logits[:8]
    allowed = jnp.where(mask[...] > 0.5, jnp.exp(jnp.where(mask[...] > 0.5, logits, 0.0)), 0.0)
    totals = jnp.sum(allowed, axis=1, keepdims=True)
    picked = jnp.sum(jnp.where(pick[...] > 0.5, logits, 0.0), axis=1, keepdims=True)
    lane = iota((16, 128), 1)
    for i in range(8):
        value = jnp.where(lane < 2, totals[i : i + 1], picked[i : i + 1])
        sent[i * 16 : (i + 1) * 16, :] = place[i * 16 : (i + 1) * 16, :] * value


def struct(shape, dtype):
    return jax.ShapeDtypeStruct(shape, dtype)


def far(*arrays):
    return [pltpu.with_memory_space_constraint(array, pltpu.HBM) for array in arrays]


def params(mib):
    return pltpu.CompilerParams(vmem_limit_bytes=mib * 1024 * 1024)


def body(
    x_new,
    z_gate,
    bc_new,
    dt_raw,
    conv_x,
    conv_bc,
    conv_x_weight,
    conv_bc_weight,
    dt_bias,
    a_log,
    d_skip,
    ssm_state,
    norm_gain,
    out_weight,
    residual,
    final_gain,
    vocab_weight,
    tile_ids,
    tile_valid,
    sampled,
):
    tab = jnp.concatenate([tile_ids, tile_valid, sampled[:, None]], axis=1)
    sel, mask, pick, place = pl.pallas_call(
        tables_kernel,
        out_shape=(
            struct((BLOCK_ROWS, DEVICES), f32),
            struct((8, SHARD), f32),
            struct((8, SHARD), f32),
            struct((DEVICES, 128), f32),
        ),
        in_specs=[VMEM],
        out_specs=(VMEM,) * 4,
        compiler_params=params(8),
        name="tables",
    )(tab)
    small = lambda *shape: pltpu.VMEM(shape, f32)
    half = lambda *shape: pltpu.VMEM(shape, bf16)
    new_state, sent = pl.pallas_call(
        ssm_kernel,
        out_shape=(struct((ROWS, CHAN, STATE), bf16), struct((BATCH, LINES + 16, 128), bf16)),
        in_specs=[HBM] * 14,
        out_specs=(HBM, VMEM),
        scratch_shapes=[
            half(ROWS, CHAN), half(ROWS, CHAN), half(ROWS, STATE), half(ROWS, STATE), small(ROWS, HEADS),
            half(3, ROWS, CHAN), half(3, ROWS, STATE), half(3, ROWS, STATE),
            small(4, CHAN), small(4, STATE), small(4, STATE),
            small(1, HEADS), small(1, HEADS), small(1, HEADS), small(1, CHAN), small(4, 128),
            half(ROWS, CHAN, STATE), half(ROWS, CHAN, STATE), small(ROWS, CHAN), small(ROWS, HEADS),
            half(CHAN, 3 * ROWS), small(3 * ROWS, STATE), small(3 * ROWS, STATE),
            pltpu.SemaphoreType.DMA((16,)), pltpu.SemaphoreType.DMA((ROWS,)), pltpu.SemaphoreType.DMA((ROWS,)),
        ],
        compiler_params=params(40),
        name="ssm",
    )(
        *far(x_new, z_gate, bc_new, dt_raw, jnp.swapaxes(conv_x, 0, 1), jnp.swapaxes(conv_bc, 0, 1),
        conv_x_weight, conv_bc_weight, dt_bias[None, :], a_log[None, :], d_skip[None, :], ssm_state.reshape(ROWS, CHAN, STATE),
        norm_gain[None, :], final_gain.reshape(4, 128))
    )
    got = lax.all_to_all(sent, "batch", 0, 0, tiled=True)
    sent, gain_all = pl.pallas_call(
        project_kernel,
        out_shape=(struct((TENSOR, BLOCK_ROWS, COLS + 128), bf16), struct((BATCH * 4, 128), f32)),
        in_specs=[VMEM] * 3,
        out_specs=(VMEM,) * 2,
        scratch_shapes=[half(BATCH * ROWS, CHAN)],
        compiler_params=params(16),
        name="project",
    )(got, out_weight, norm_gain[None, :])
    got = lax.all_to_all(sent, "tensor", 0, 0, tiled=True)
    layer_out, sent = pl.pallas_call(
        layer_kernel,
        out_shape=(struct((BLOCK_ROWS, COLS), bf16), struct((DEVICES * 4, 128), bf16)),
        in_specs=[VMEM] * 3,
        out_specs=(VMEM,) * 2,
        scratch_shapes=[small(DEVICES * 4, 128)],
        compiler_params=params(8),
        name="layer",
    )(got, residual, sel)
    got = lax.all_to_all(sent.reshape(DEVICES, 4, 128), ("batch", "tensor"), 0, 0, tiled=True)
    sent = pl.pallas_call(
        logits_kernel,
        out_shape=struct((DEVICES, 128), f32),
        in_specs=[VMEM] * 5 + [HBM],
        out_specs=VMEM,
        scratch_shapes=[
            small(DEVICES * 4, 128),
            half(16, D),
            half(SHARD, D),
            pltpu.SemaphoreType.DMA((8,)),
        ],
        compiler_params=params(24),
        name="logits",
    )(got.reshape(DEVICES * 4, 128), gain_all, mask, pick, place, *far(vocab_weight))
    got = lax.all_to_all(sent.reshape(DEVICES, 1, 128), ("batch", "tensor"), 0, 0, tiled=True)
    sums = jnp.sum(got, axis=(0, 1))
    token_logprob = sums[2:4] - jnp.log(sums[0:2])
    return (new_state.reshape(ROWS, HEADS, HEAD_DIM, STATE), layer_out, token_logprob)


def solution(mesh):
    return jax.shard_map(
        body,
        mesh=mesh,
        in_specs=(
            P("batch", "tensor"),
            P("batch", "tensor"),
            P("batch", None),
            P("batch", "tensor"),
            P("batch", None, "tensor"),
            P("batch", None, None),
            P(None, "tensor"),
            P(),
            P("tensor"),
            P("tensor"),
            P("tensor"),
            P("batch", "tensor", None, None),
            P("tensor"),
            P("tensor", "batch"),
            P("tensor", "batch"),
            P("batch"),
            P(("batch", "tensor"), None),
            P(),
            P(),
            P(),
        ),
        out_specs=(P("batch", "tensor", None, None), P("tensor", "batch"), P(("batch", "tensor"))),
        check_vma=False,
    )
```

```python
import functools

import jax
import jax.numpy as jnp
from jax import lax
from jax.experimental import pallas as pl
from jax.experimental.pallas import tpu as pltpu
from jax.sharding import PartitionSpec as P

D = 8192
HEAD_DIM = 64
STATE = 256
GROUP_HEADS = 32
GROUPS = 4
TILE = 128
TILES_DEV = 4
BLOCK_ROWS = 32

ROWS = 16
CHAN = 1024
HEADS = 16
KB = CHAN // 128
LINES = KB * ROWS
COLS = 512
BATCH = 16
TENSOR = 8
DEVICES = BATCH * TENSOR
SHARD = TILES_DEV * TILE
STEP = 4
GROUP_ROWS = 4

epsilon = 1e-05
f32 = jnp.float32
bf16 = jnp.bfloat16
HBM = pl.BlockSpec(memory_space=pltpu.HBM)
ANY = pl.BlockSpec(memory_space=pl.ANY)
VMEM = pl.BlockSpec(memory_space=pltpu.VMEM)
HIGHEST = lax.Precision.HIGHEST


def split(value, parts):
    pieces = []
    for _ in range(parts):
        piece = value.astype(bf16)
        pieces.append(piece)
        value = value - piece.astype(f32)
    return pieces


def silu(value):
    return value / (1.0 + jnp.exp(-value))


def dot(a, b, contract=((1,), (0,)), precision=None):
    return lax.dot_general(a, b, (contract, ((), ())), precision=precision, preferred_element_type=f32)


def iota(shape, dim):
    return lax.broadcasted_iota(jnp.int32, shape, dim)


def tables_kernel(tab, sel, mask, pick, place, home):
    tensor = lax.axis_index("tensor")
    shard = lax.axis_index("batch") * TENSOR + tensor
    lanes = iota((BLOCK_ROWS, DEVICES), 1)
    for n in range(4):
        block = (2 * n + tensor % 2) * BLOCK_ROWS
        own = tab[pl.ds(pl.multiple_of(block, BLOCK_ROWS), BLOCK_ROWS), :]
        used = jnp.zeros((BLOCK_ROWS, DEVICES), f32)
        for slot in range(4):
            tiles = own[:, slot : slot + 1]
            valid = own[:, 4 + slot : 5 + slot]
            hit = jnp.where(valid == 1, tiles >> 2, -1) == lanes
            used = jnp.where(hit, 1.0, used)
        sel[n] = used
    rows = DEVICES * 2
    whole = tab[...]
    tile = shard * TILES_DEV + iota((rows, SHARD), 1) // TILE
    held = jnp.zeros((rows, SHARD), f32)
    mine = jnp.zeros((rows, 1), f32)
    for slot in range(4):
        tiles = jnp.where(whole[:, 4 + slot : 5 + slot] == 1, whole[:, slot : slot + 1], -1)
        held = jnp.where(tiles == tile, 1.0, held)
        mine = jnp.where((tiles >> 2) == shard, 1.0, mine)
    chosen = jnp.where(whole[:, 8:9] == shard * SHARD + iota((rows, SHARD), 1), 1.0, 0.0)
    order = iota((8, rows), 0)
    order = 2 * (order % 4) + order // 4
    block = jnp.where(iota((8, rows), 1) // BLOCK_ROWS == order, 1.0, 0.0).astype(bf16)
    mask[...] = dot(block, held.astype(bf16))
    pick[...] = dot(block, chosen.astype(bf16))
    lane = iota((rows, 128), 1)
    parity = (lane % 2 == iota((rows, 128), 0) % 2) & (lane < 12)
    spread = jnp.where(parity, mine, 0.0).astype(bf16)
    pairs = jnp.where(iota((DEVICES, rows), 1) // 2 == iota((DEVICES, rows), 0), 1.0, 0.0).astype(bf16)
    place[...] = dot(pairs, spread)
    own = tab[pl.ds(pl.multiple_of(tensor * BLOCK_ROWS, BLOCK_ROWS), BLOCK_ROWS), :]
    line = iota((BLOCK_ROWS, DEVICES * 8), 1)
    for q in range(4):
        found = line == (own[:, 8:9] // SHARD) * 8 + q
        home[q * BLOCK_ROWS : (q + 1) * BLOCK_ROWS, :] = jnp.where(found, 1.0, 0.0).astype(bf16)
    line = iota((16, DEVICES * 8), 1)
    found = (line % 8 == 4) & (iota((16, DEVICES * 8), 0) == 0)
    home[DEVICES : DEVICES + 16, :] = jnp.where(found, 1.0, 0.0).astype(bf16)


def ssm_kernel(
    x_new, z_gate, bc_new, dt_raw, conv_x, conv_bc, wx, wbc, dt_bias, a_log, d_skip, state, gain, final_gain,
    sent, sx_t, b_pieces, decay_out,
    x_v, z_v, b_v, c_v, dt_v, cx_v, cb_v, cc_v, wx_v, wb_v, wc_v, bias_v, alog_v, skip_v, gain_v, fg_v,
    state_v, acc, c_t, small_sem, in_sem,
):
    group = lax.axis_index("tensor") // 2
    first = pl.ds(pl.multiple_of(group * STATE, STATE), STATE)
    second = pl.ds(pl.multiple_of((GROUPS + group) * STATE, STATE), STATE)
    pairs = [
        (bc_new.at[:, second], c_v), (conv_bc.at[:, :, second], cc_v), (wbc.at[:, second], wc_v),
        (dt_raw, dt_v), (dt_bias, bias_v), (a_log, alog_v), (d_skip, skip_v),
        (conv_x, cx_v), (x_new, x_v), (wx, wx_v),
        (bc_new.at[:, first], b_v), (conv_bc.at[:, :, first], cb_v), (wbc.at[:, first], wb_v),
        (z_gate, z_v), (gain, gain_v), (final_gain, fg_v),
    ]
    copies = [pltpu.make_async_copy(src, dst, small_sem.at[n]) for n, (src, dst) in enumerate(pairs)]
    for copy in copies:
        copy.start()

    def rows_in(n):
        part = pl.ds(n * STEP, STEP)
        return pltpu.make_async_copy(state.at[part], state_v.at[part], in_sem.at[n])

    for n in range(ROWS // STEP):
        rows_in(n).start()

    def conv(window, newest, weight):
        total = newest[...].astype(f32) * weight[3:4, :]
        for k in range(3):
            total = total + window[k].astype(f32) * weight[k : k + 1, :]
        return silu(total)

    for copy in copies[:3]:
        copy.wait()
    c_out = conv(cc_v, c_v, wc_v)
    pieces = [piece.astype(f32) for piece in split(c_out, 3)]
    c_t[...] = jnp.concatenate(pieces + [jnp.zeros((128 - 3 * ROWS, STATE), f32)], 0).T.astype(bf16)
    acc[...] = jnp.zeros_like(acc)
    column = iota((128, 128), 1) % ROWS

    def some_rows(n, carry):
        rows_in(n).wait()
        for m in range(CHAN // 128):
            part = slice(m * 128, (m + 1) * 128)
            total = acc[part, :]
            for k in range(STEP):
                r = n * STEP + k
                total = jnp.where(column == r, dot(state_v[r, part, :], c_t[...]), total)
            acc[part, :] = total
        return carry

    lax.fori_loop(0, ROWS // STEP, some_rows, 0)
    for copy in copies[3:]:
        copy.wait()
    raw = dt_v[...] + bias_v[...]
    step = jnp.maximum(raw, 0.0) + jnp.log1p(jnp.exp(-jnp.abs(raw)))
    decay = jnp.exp(-jnp.exp(alog_v[...]) * step)
    decay_out[...] = decay
    spread = jnp.where(iota((HEADS, CHAN), 1) // HEAD_DIM == iota((HEADS, CHAN), 0), 1.0, 0.0)
    wide = dot(jnp.concatenate([step, decay, jnp.broadcast_to(skip_v[...], (8, HEADS))], 0), spread, precision=HIGHEST)
    step_c, decay_c, skip_c = wide[:ROWS], wide[ROWS : 2 * ROWS], wide[2 * ROWS : 2 * ROWS + 1]
    conv_out = conv(cx_v, x_v, wx_v)
    b_in = conv(cb_v, b_v, wb_v)
    sx = step_c * conv_out
    sx_hi, sx_lo = split(sx, 2)
    sx_t[...] = jnp.concatenate([sx_hi.astype(f32), sx_lo.astype(f32), sx_hi.astype(f32)], 0).T.astype(bf16)
    b_hi, b_lo = split(b_in, 2)
    b_pieces[...] = jnp.concatenate([b_hi.astype(f32), b_hi.astype(f32), b_lo.astype(f32)], 0)
    inner = jnp.sum(b_in * c_out, axis=1, keepdims=True)
    total = acc[...].T
    total = total[:ROWS] + total[ROWS : 2 * ROWS] + total[2 * ROWS : 3 * ROWS]
    ssm_out = decay_c * total + sx * inner + skip_c * conv_out
    gated = ssm_out * silu(z_v[...].astype(f32))
    scaled = (gated * gain_v[...]).astype(bf16)
    hi, mid, lo = [piece.astype(f32) for piece in split(fg_v[...], 3)]
    tail = jnp.concatenate([hi, mid, lo, jnp.zeros_like(hi)], 0).astype(bf16)
    for b in range(BATCH):
        for k in range(KB):
            sent[b, k * ROWS : (k + 1) * ROWS, :] = scaled[:, k * 128 : (k + 1) * 128]
        sent[b, LINES : LINES + 16, :] = tail


def state_kernel(state, sx_t, b_pieces, decay, new_state, done, state_v, out_v, in_sem, out_sem):
    done[...] = jnp.zeros_like(done)

    def rows_in(n):
        part = pl.ds(n * GROUP_ROWS, GROUP_ROWS)
        return pltpu.make_async_copy(state.at[part], state_v.at[part], in_sem.at[n])

    def rows_out(n):
        part = pl.ds(n * GROUP_ROWS, GROUP_ROWS)
        return pltpu.make_async_copy(out_v.at[part], new_state.at[part], out_sem.at[n])

    steps = ROWS // GROUP_ROWS
    for n in range(steps):
        rows_in(n).start()

    def some_rows(n, carry):
        rows_in(n).wait()
        for k in range(GROUP_ROWS):
            r = n * GROUP_ROWS + k
            on_row = iota((3 * ROWS, STATE), 0) % ROWS == r
            b_row = jnp.where(on_row, b_pieces[...], 0.0).astype(bf16)
            scale = decay[pl.ds(r, 1), :]
            for m in range(CHAN // 128):
                outer = dot(sx_t[m * 128 : (m + 1) * 128, :], b_row)
                for half in range(2):
                    head = 2 * m + half
                    rows = slice(head * HEAD_DIM, (head + 1) * HEAD_DIM)
                    fresh = scale[:, head : head + 1] * state_v[r, rows, :].astype(f32)
                    out_v[r, rows, :] = (fresh + outer[half * HEAD_DIM : (half + 1) * HEAD_DIM]).astype(bf16)
        rows_out(n).start()
        return carry

    lax.fori_loop(0, steps, some_rows, 0)

    def finish(n, carry):
        rows_out(n).wait()
        return carry

    lax.fori_loop(0, steps, finish, 0)


def project_kernel(got, weight, gain, tables_done, state_done, sent, kept, final_gain, lhs):
    core = lax.axis_index("tensor") % 2
    for side in range(2):
        parity = core if side else 1 - core
        for n in range(4):
            for e in range(2):
                b = 4 * n + 2 * parity + e
                to = (side * 8 + n * 2 + e) * ROWS
                for k in range(KB):
                    lhs[to : to + ROWS, k * 128 : (k + 1) * 128] = got[b, k * ROWS : (k + 1) * ROWS, :]
    for b in range(BATCH):
        pieces = got[b, LINES : LINES + 16, :].astype(f32)
        final_gain[b * 4 : b * 4 + 4, :] = pieces[0:4] + pieces[4:8] + pieces[8:12]
    inverse = 1.0 / gain[...]
    inverse = inverse * inverse
    lane = iota((128, 128), 1)
    for side, out in enumerate((sent, kept)):
        rows = lhs[side * 128 : (side + 1) * 128, :]
        product = dot(rows, weight[...])
        wide = rows.astype(f32)
        square = jnp.sum(wide * wide * inverse, axis=1, keepdims=True)
        hi, mid, lo = [piece.astype(f32) for piece in split(square, 3)]
        tail = jnp.where(lane == 0, hi, jnp.where(lane == 1, mid, jnp.where(lane == 2, lo, 0.0)))
        out[:, :COLS] = product.astype(out.dtype)
        out[:, COLS:] = tail.astype(out.dtype)


def merge_kernel(got, kept, residual, sel, sent, total, lines):
    x = lax.axis_index("tensor") // 2
    both = got[...].astype(f32) + kept[...]
    square = jnp.sum(both[:, COLS:], axis=1, keepdims=True)
    total[...] = both[:, :COLS] * lax.rsqrt(square / (GROUP_HEADS * HEAD_DIM) + epsilon)
    mine = pl.ds(pl.multiple_of(x * BLOCK_ROWS, BLOCK_ROWS), BLOCK_ROWS)
    total[mine, :] = total[mine, :] + residual[...].astype(f32)
    for n in range(4):
        rows = total[n * BLOCK_ROWS : (n + 1) * BLOCK_ROWS, :].astype(bf16)
        picked = dot(sel[n].astype(bf16), rows, ((0,), (0,)))
        for q in range(4):
            lines[pl.ds(n * 4 + q, DEVICES, stride=16), :] = picked[:, q * 128 : (q + 1) * 128]
    sent[...] = lines[...].astype(bf16)


def logits_kernel(got, gain, mask, pick, place, vocab, sent, lines, lhs):
    square = jnp.zeros((8, 128), f32)
    logits = jnp.zeros((16, SHARD), f32)
    for b in range(BATCH):
        for c in range(2):
            value = jnp.zeros((16, 128), f32)
            for x in range(4):
                start = ((b * 4 + x) * 2 + c) * 16
                value = value + got[start : start + 16, :].astype(f32)
            lines[(b * 2 + c) * 16 : (b * 2 + c + 1) * 16, :] = value.astype(bf16).astype(f32)
        for q in range(4):
            n = b * 4 + q
            value = lines[pl.ds(b * 32 + q, 8, stride=4), :]
            square = square + value * value
            value = value * gain[n : n + 1, :]
            lhs[:, n * 128 : (n + 1) * 128] = jnp.concatenate([value, jnp.zeros_like(value)], 0).astype(bf16)
        part = slice(b * COLS, (b + 1) * COLS)
        logits = logits + dot(lhs[:, part], vocab[:, part], ((1,), (1,)))
    logits = logits[:8] * lax.rsqrt(jnp.sum(square, axis=1, keepdims=True) / D + epsilon)
    allowed = jnp.where(mask[...] > 0.5, jnp.exp(jnp.where(mask[...] > 0.5, logits, 0.0)), 0.0)
    totals = jnp.sum(allowed, axis=1, keepdims=True)
    picked = jnp.sum(jnp.where(pick[...] > 0.5, logits, 0.0), axis=1, keepdims=True)
    lane = iota((8, 128), 1)
    value = jnp.zeros((8, 128), f32)
    for n, (left, right) in enumerate(zip(split(totals, 3), split(picked, 3))):
        pair = jnp.where(lane % 4 < 2, left.astype(f32), right.astype(f32))
        value = jnp.where(lane // 4 == n, pair, value)
    sub = iota((8, 128), 0)
    for d in range(DEVICES):
        b, t = d // TENSOR, d % TENSOR
        i = d // 16
        row = b * 32 + ((t % 2) * 4 + t // 2) * 4
        j = (i % 2) * 4 + i // 2
        features = lines[row : row + 8, :]
        note = place[d : d + 1, :] * value[j : j + 1, :]
        group = jnp.where(sub < 4, features, jnp.where(sub == 4, note, 0.0))
        if d % 2 == 0:
            first = group
        else:
            sent[(d - 1) * 8 : (d + 1) * 8, :] = jnp.concatenate([first, group], 0).astype(bf16)


def finish_kernel(got, home, layer_out, token):
    found = dot(home[...], got[...])
    for q in range(4):
        layer_out[:, q * 128 : (q + 1) * 128] = found[q * BLOCK_ROWS : (q + 1) * BLOCK_ROWS].astype(bf16)
    sums = found[DEVICES : DEVICES + 1, :]
    totals = sums[:, 0:2] + sums[:, 4:6] + sums[:, 8:10]
    picked = sums[:, 2:4] + sums[:, 6:8] + sums[:, 10:12]
    token[...] = picked - jnp.log(totals)


def struct(shape, dtype):
    return jax.ShapeDtypeStruct(shape, dtype)


def far(*arrays):
    return [pltpu.with_memory_space_constraint(array, pltpu.HBM) for array in arrays]


def near(array):
    return pltpu.with_memory_space_constraint(array, pltpu.VMEM)


def params(mib):
    return pltpu.CompilerParams(vmem_limit_bytes=mib * 1024 * 1024)


def body(
    x_new,
    z_gate,
    bc_new,
    dt_raw,
    conv_x,
    conv_bc,
    conv_x_weight,
    conv_bc_weight,
    dt_bias,
    a_log,
    d_skip,
    ssm_state,
    norm_gain,
    out_weight,
    residual,
    final_gain,
    vocab_weight,
    tile_ids,
    tile_valid,
    sampled,
):
    tab = jnp.concatenate([tile_ids, tile_valid, sampled[:, None]], axis=1)
    sel, mask, pick, place, home = pl.pallas_call(
        tables_kernel,
        out_shape=(
            struct((4, BLOCK_ROWS, DEVICES), f32),
            struct((8, SHARD), f32),
            struct((8, SHARD), f32),
            struct((DEVICES, 128), f32),
            struct((DEVICES + 16, DEVICES * 8), bf16),
        ),
        in_specs=[VMEM],
        out_specs=(VMEM,) * 5,
        compiler_params=params(8),
        name="tables",
    )(tab)
    small = lambda *shape: pltpu.VMEM(shape, f32)
    half = lambda *shape: pltpu.VMEM(shape, bf16)
    state = ssm_state.reshape(ROWS, CHAN, STATE)
    sent, sx_t, b_pieces, decay = pl.pallas_call(
        ssm_kernel,
        out_shape=(
            struct((BATCH, LINES + 16, 128), bf16),
            struct((CHAN, 3 * ROWS), bf16),
            struct((3 * ROWS, STATE), f32),
            struct((ROWS, HEADS), f32),
        ),
        in_specs=[HBM] * 14,
        out_specs=(VMEM,) * 4,
        scratch_shapes=[
            half(ROWS, CHAN), half(ROWS, CHAN), half(ROWS, STATE), half(ROWS, STATE), small(ROWS, HEADS),
            half(3, ROWS, CHAN), half(3, ROWS, STATE), half(3, ROWS, STATE),
            small(4, CHAN), small(4, STATE), small(4, STATE),
            small(1, HEADS), small(1, HEADS), small(1, HEADS), small(1, CHAN), small(4, 128),
            half(ROWS, CHAN, STATE), small(CHAN, 128), half(STATE, 128),
            pltpu.SemaphoreType.DMA((16,)), pltpu.SemaphoreType.DMA((ROWS // STEP,)),
        ],
        compiler_params=params(24),
        name="ssm",
    )(
        *far(x_new, z_gate, bc_new, dt_raw, jnp.swapaxes(conv_x, 0, 1), jnp.swapaxes(conv_bc, 0, 1),
        conv_x_weight, conv_bc_weight, dt_bias[None, :], a_log[None, :], d_skip[None, :], state,
        norm_gain[None, :], final_gain.reshape(4, 128))
    )
    new_state, state_done = pl.pallas_call(
        state_kernel,
        out_shape=(struct((ROWS, CHAN, STATE), bf16), struct((8, 128), f32)),
        in_specs=[HBM] + [VMEM] * 3,
        out_specs=(HBM, VMEM),
        scratch_shapes=[
            half(ROWS, CHAN, STATE),
            half(ROWS, CHAN, STATE),
            pltpu.SemaphoreType.DMA((ROWS // GROUP_ROWS,)),
            pltpu.SemaphoreType.DMA((ROWS // GROUP_ROWS,)),
        ],
        compiler_params=params(24),
        cost_estimate=pl.CostEstimate(flops=10**9, bytes_accessed=2 * ROWS * CHAN * STATE * 2, transcendentals=0),
        name="state",
    )(*far(state), sx_t, b_pieces, decay)
    got = lax.all_to_all(sent, "batch", 0, 0, tiled=True)
    sent, kept, gain_all = pl.pallas_call(
        project_kernel,
        out_shape=(
            struct((128, COLS + 128), bf16),
            struct((128, COLS + 128), f32),
            struct((BATCH * 4, 128), f32),
        ),
        in_specs=[VMEM] * 3 + [ANY] * 2,
        out_specs=(VMEM,) * 3,
        scratch_shapes=[half(BATCH * ROWS, CHAN)],
        compiler_params=params(16),
        cost_estimate=pl.CostEstimate(flops=5 * 10**9, bytes_accessed=10**7, transcendentals=0),
        name="project",
    )(got, out_weight, norm_gain[None, :], sel, state_done)
    got = lax.ppermute(sent, "tensor", [(t, t ^ 1) for t in range(TENSOR)])
    sent = pl.pallas_call(
        merge_kernel,
        out_shape=struct((DEVICES * 16, 128), bf16),
        in_specs=[VMEM] * 4,
        out_specs=VMEM,
        scratch_shapes=[small(128, COLS), small(DEVICES * 16, 128)],
        compiler_params=params(8),
        cost_estimate=pl.CostEstimate(flops=5 * 10**9, bytes_accessed=10**7, transcendentals=0),
        name="merge",
    )(got, kept, residual, sel)
    got = lax.all_to_all(sent.reshape(DEVICES, 16, 128), ("batch", "tensor"), 0, 0, tiled=True)
    sent = pl.pallas_call(
        logits_kernel,
        out_shape=struct((DEVICES * 8, 128), bf16),
        in_specs=[VMEM] * 6,
        out_specs=VMEM,
        scratch_shapes=[
            small(DEVICES * 4 + 8, 128),
            half(16, D),
        ],
        compiler_params=params(16),
        name="logits",
    )(got.reshape(DEVICES * 16, 128), gain_all, mask, pick, place, near(vocab_weight))
    got = lax.all_to_all(sent.reshape(DEVICES, 8, 128), ("batch", "tensor"), 0, 0, tiled=True)
    layer_out, token_logprob = pl.pallas_call(
        finish_kernel,
        out_shape=(struct((BLOCK_ROWS, COLS), bf16), struct((1, 2), f32)),
        in_specs=[VMEM] * 2,
        out_specs=(VMEM,) * 2,
        compiler_params=params(4),
        name="finish",
    )(got.reshape(DEVICES * 8, 128), home)
    token_logprob = token_logprob.reshape(2)
    return (new_state.reshape(ROWS, HEADS, HEAD_DIM, STATE), layer_out, token_logprob)


def solution(mesh):
    return jax.shard_map(
        body,
        mesh=mesh,
        in_specs=(
            P("batch", "tensor"),
            P("batch", "tensor"),
            P("batch", None),
            P("batch", "tensor"),
            P("batch", None, "tensor"),
            P("batch", None, None),
            P(None, "tensor"),
            P(),
            P("tensor"),
            P("tensor"),
            P("tensor"),
            P("batch", "tensor", None, None),
            P("tensor"),
            P("tensor", "batch"),
            P("tensor", "batch"),
            P("batch"),
            P(("batch", "tensor"), None),
            P(),
            P(),
            P(),
        ),
        out_specs=(P("batch", "tensor", None, None), P("tensor", "batch"), P(("batch", "tensor"))),
        check_vma=False,
    )
```

```python
import functools

import jax
import jax.numpy as jnp
from jax import lax
from jax.experimental import pallas as pl
from jax.experimental.pallas import tpu as pltpu
from jax.sharding import PartitionSpec as P

D = 8192
HEAD_DIM = 64
STATE = 256
GROUP_HEADS = 32
GROUPS = 4
TILE = 128
TILES_DEV = 4
BLOCK_ROWS = 32

ROWS = 16
CHAN = 1024
HEADS = 16
KB = CHAN // 128
LINES = KB * ROWS
COLS = 512
BATCH = 16
TENSOR = 8
DEVICES = BATCH * TENSOR
SHARD = TILES_DEV * TILE
STEP = 4
GROUP_ROWS = 4

epsilon = 1e-05
f32 = jnp.float32
bf16 = jnp.bfloat16
HBM = pl.BlockSpec(memory_space=pltpu.HBM)
ANY = pl.BlockSpec(memory_space=pl.ANY)
VMEM = pl.BlockSpec(memory_space=pltpu.VMEM)
HIGHEST = lax.Precision.HIGHEST


def split(value, parts):
    pieces = []
    for _ in range(parts):
        piece = value.astype(bf16)
        pieces.append(piece)
        value = value - piece.astype(f32)
    return pieces


def silu(value):
    return value / (1.0 + jnp.exp(-value))


def dot(a, b, contract=((1,), (0,)), precision=None):
    return lax.dot_general(a, b, (contract, ((), ())), precision=precision, preferred_element_type=f32)


def iota(shape, dim):
    return lax.broadcasted_iota(jnp.int32, shape, dim)


def tables_kernel(tab, sel, mask, pick, place, home):
    tensor = lax.axis_index("tensor")
    shard = lax.axis_index("batch") * TENSOR + tensor
    lanes = iota((BLOCK_ROWS, DEVICES), 1)
    for n in range(4):
        block = (2 * n + tensor % 2) * BLOCK_ROWS
        own = tab[pl.ds(pl.multiple_of(block, BLOCK_ROWS), BLOCK_ROWS), :]
        used = jnp.zeros((BLOCK_ROWS, DEVICES), f32)
        for slot in range(4):
            tiles = own[:, slot : slot + 1]
            valid = own[:, 4 + slot : 5 + slot]
            hit = jnp.where(valid == 1, tiles >> 2, -1) == lanes
            used = jnp.where(hit, 1.0, used)
        sel[n] = used
    rows = DEVICES * 2
    whole = tab[...]
    tile = shard * TILES_DEV + iota((rows, SHARD), 1) // TILE
    held = jnp.zeros((rows, SHARD), f32)
    mine = jnp.zeros((rows, 1), f32)
    for slot in range(4):
        tiles = jnp.where(whole[:, 4 + slot : 5 + slot] == 1, whole[:, slot : slot + 1], -1)
        held = jnp.where(tiles == tile, 1.0, held)
        mine = jnp.where((tiles >> 2) == shard, 1.0, mine)
    chosen = jnp.where(whole[:, 8:9] == shard * SHARD + iota((rows, SHARD), 1), 1.0, 0.0)
    order = iota((8, rows), 0)
    order = 2 * (order % 4) + order // 4
    block = jnp.where(iota((8, rows), 1) // BLOCK_ROWS == order, 1.0, 0.0).astype(bf16)
    mask[...] = dot(block, held.astype(bf16))
    pick[...] = dot(block, chosen.astype(bf16))
    lane = iota((rows, 128), 1)
    parity = (lane % 2 == iota((rows, 128), 0) % 2) & (lane < 12)
    spread = jnp.where(parity, mine, 0.0).astype(bf16)
    pairs = jnp.where(iota((DEVICES, rows), 1) // 2 == iota((DEVICES, rows), 0), 1.0, 0.0).astype(bf16)
    place[...] = dot(pairs, spread)
    own = tab[pl.ds(pl.multiple_of(tensor * BLOCK_ROWS, BLOCK_ROWS), BLOCK_ROWS), :]
    line = iota((BLOCK_ROWS, DEVICES * 8), 1)
    for q in range(4):
        found = line == (own[:, 8:9] // SHARD) * 8 + q
        home[q * BLOCK_ROWS : (q + 1) * BLOCK_ROWS, :] = jnp.where(found, 1.0, 0.0).astype(bf16)
    line = iota((16, DEVICES * 8), 1)
    found = (line % 8 == 4) & (iota((16, DEVICES * 8), 0) == 0)
    home[DEVICES : DEVICES + 16, :] = jnp.where(found, 1.0, 0.0).astype(bf16)


def ssm_kernel(
    x_new, z_gate, bc_new, dt_raw, conv_x, conv_bc, wx, wbc, dt_bias, a_log, d_skip, state, gain, final_gain,
    sent, sx_t, b_pieces, decay_out,
    x_v, z_v, b_v, c_v, dt_v, cx_v, cb_v, cc_v, wx_v, wb_v, wc_v, bias_v, alog_v, skip_v, gain_v, fg_v,
    state_v, acc, c_t, c_f, small_sem, in_sem,
):
    group = lax.axis_index("tensor") // 2
    first = pl.ds(pl.multiple_of(group * STATE, STATE), STATE)
    second = pl.ds(pl.multiple_of((GROUPS + group) * STATE, STATE), STATE)
    pairs = [
        (bc_new.at[:, second], c_v), (conv_bc.at[:, :, second], cc_v), (wbc.at[:, second], wc_v),
        (dt_raw, dt_v), (dt_bias, bias_v), (a_log, alog_v), (d_skip, skip_v),
        (conv_x, cx_v), (x_new, x_v), (wx, wx_v),
        (bc_new.at[:, first], b_v), (conv_bc.at[:, :, first], cb_v), (wbc.at[:, first], wb_v),
        (z_gate, z_v), (gain, gain_v), (final_gain, fg_v),
    ]
    copies = [pltpu.make_async_copy(src, dst, small_sem.at[n]) for n, (src, dst) in enumerate(pairs)]
    for copy in copies:
        copy.start()

    def rows_in(n):
        part = pl.ds(n * STEP, STEP)
        return pltpu.make_async_copy(state.at[part], state_v.at[part], in_sem.at[n])

    for n in range(ROWS // STEP):
        rows_in(n).start()

    def conv(window, newest, weight):
        total = newest[...].astype(f32) * weight[3:4, :]
        for k in range(3):
            total = total + window[k].astype(f32) * weight[k : k + 1, :]
        return silu(total)

    for copy in copies[:3]:
        copy.wait()
    c_out = conv(cc_v, c_v, wc_v)
    pieces = [piece.astype(f32) for piece in split(c_out, 3)]
    c_t[...] = jnp.concatenate(pieces + [jnp.zeros((128 - 3 * ROWS, STATE), f32)], 0).T.astype(bf16)
    acc[...] = jnp.zeros_like(acc)
    c_f[...] = c_out
    lane = iota((128, 128), 1)
    column = lane % ROWS

    def some_rows(n, carry):
        rows_in(n).wait()
        for m in range(CHAN // 128):
            part = slice(m * 128, (m + 1) * 128)
            total = acc[part, :]
            for k in range(STEP):
                r = n * STEP + k
                if k < 2:
                    total = jnp.where(column == r, dot(state_v[r, part, :], c_t[...]), total)
                else:
                    weighed = state_v[r, part, :].astype(f32) * c_f[pl.ds(r, 1), :]
                    total = jnp.where(lane == r, jnp.sum(weighed, axis=1, keepdims=True), total)
            acc[part, :] = total
        return carry

    lax.fori_loop(0, 3, some_rows, 0)
    for copy in copies[3:]:
        copy.wait()
    raw = dt_v[...] + bias_v[...]
    step = jnp.maximum(raw, 0.0) + jnp.log1p(jnp.exp(-jnp.abs(raw)))
    decay = jnp.exp(-jnp.exp(alog_v[...]) * step)
    decay_out[...] = decay
    spread = jnp.where(iota((HEADS, CHAN), 1) // HEAD_DIM == iota((HEADS, CHAN), 0), 1.0, 0.0)
    wide = dot(jnp.concatenate([step, decay, jnp.broadcast_to(skip_v[...], (8, HEADS))], 0), spread, precision=HIGHEST)
    step_c, decay_c, skip_c = wide[:ROWS], wide[ROWS : 2 * ROWS], wide[2 * ROWS : 2 * ROWS + 1]
    conv_out = conv(cx_v, x_v, wx_v)
    b_in = conv(cb_v, b_v, wb_v)
    sx = step_c * conv_out
    sx_hi, sx_lo = split(sx, 2)
    sx_t[...] = jnp.concatenate([sx_hi.astype(f32), sx_lo.astype(f32), sx_hi.astype(f32)], 0).T.astype(bf16)
    b_hi, b_lo = split(b_in, 2)
    b_pieces[...] = jnp.concatenate([b_hi.astype(f32), b_hi.astype(f32), b_lo.astype(f32)], 0)
    gate = silu(z_v[...].astype(f32)) * gain_v[...]
    lax.fori_loop(3, ROWS // STEP, some_rows, 0)
    inner = jnp.sum(b_in * c_out, axis=1, keepdims=True)
    total = acc[...].T
    total = total[:ROWS] + total[ROWS : 2 * ROWS] + total[2 * ROWS : 3 * ROWS]
    ssm_out = decay_c * total + sx * inner + skip_c * conv_out
    scaled = (ssm_out * gate).astype(bf16)
    hi, mid = [piece.astype(f32) for piece in split(fg_v[...], 2)]
    tail = jnp.concatenate([hi, mid], 0).astype(bf16)
    for b in range(BATCH):
        for k in range(KB):
            sent[b, k * ROWS : (k + 1) * ROWS, :] = scaled[:, k * 128 : (k + 1) * 128]
        sent[b, LINES : LINES + 8, :] = tail


def state_kernel(state, sx_t, b_pieces, decay, new_state, done, state_v, out_v, in_sem, out_sem):
    done[...] = jnp.zeros_like(done)

    def rows_in(n):
        part = pl.ds(n * GROUP_ROWS, GROUP_ROWS)
        return pltpu.make_async_copy(state.at[part], state_v.at[part], in_sem.at[n])

    def rows_out(n):
        part = pl.ds(n * GROUP_ROWS, GROUP_ROWS)
        return pltpu.make_async_copy(out_v.at[part], new_state.at[part], out_sem.at[n])

    steps = ROWS // GROUP_ROWS
    for n in range(steps):
        rows_in(n).start()

    def some_rows(n, carry):
        rows_in(n).wait()
        for k in range(GROUP_ROWS):
            r = n * GROUP_ROWS + k
            on_row = iota((3 * ROWS, STATE), 0) % ROWS == r
            b_row = jnp.where(on_row, b_pieces[...], 0.0).astype(bf16)
            scale = decay[pl.ds(r, 1), :]
            for m in range(CHAN // 128):
                outer = dot(sx_t[m * 128 : (m + 1) * 128, :], b_row)
                for half in range(2):
                    head = 2 * m + half
                    rows = slice(head * HEAD_DIM, (head + 1) * HEAD_DIM)
                    fresh = scale[:, head : head + 1] * state_v[r, rows, :].astype(f32)
                    out_v[r, rows, :] = (fresh + outer[half * HEAD_DIM : (half + 1) * HEAD_DIM]).astype(bf16)
        rows_out(n).start()
        return carry

    lax.fori_loop(0, steps, some_rows, 0)

    def finish(n, carry):
        rows_out(n).wait()
        return carry

    lax.fori_loop(0, steps, finish, 0)


def project_kernel(got, weight, gain, tables_done, state_done, sent, kept, final_gain, lhs):
    core = lax.axis_index("tensor") % 2
    for side in range(2):
        parity = core if side else 1 - core
        for n in range(4):
            for e in range(2):
                b = 4 * n + 2 * parity + e
                to = (side * 8 + n * 2 + e) * ROWS
                for k in range(KB):
                    lhs[to : to + ROWS, k * 128 : (k + 1) * 128] = got[b, k * ROWS : (k + 1) * ROWS, :]
    for b in range(BATCH):
        pieces = got[b, LINES : LINES + 8, :].astype(f32)
        final_gain[b * 4 : b * 4 + 4, :] = pieces[0:4] + pieces[4:8]
    inverse = 1.0 / gain[...]
    inverse = inverse * inverse
    lane = iota((128, 128), 1)
    for side, out in enumerate((sent, kept)):
        rows = lhs[side * 128 : (side + 1) * 128, :]
        product = dot(rows, weight[...])
        wide = rows.astype(f32)
        square = jnp.sum(wide * wide * inverse, axis=1, keepdims=True)
        hi, mid, lo = [piece.astype(f32) for piece in split(square, 3)]
        tail = jnp.where(lane == 0, hi, jnp.where(lane == 1, mid, jnp.where(lane == 2, lo, 0.0)))
        out[:, :COLS] = product.astype(out.dtype)
        out[:, COLS:] = tail.astype(out.dtype)


def merge_kernel(got, kept, residual, sel, sent, total, lines):
    x = lax.axis_index("tensor") // 2
    both = got[...].astype(f32) + kept[...]
    square = jnp.sum(both[:, COLS:], axis=1, keepdims=True)
    total[...] = both[:, :COLS] * lax.rsqrt(square / (GROUP_HEADS * HEAD_DIM) + epsilon)
    mine = pl.ds(pl.multiple_of(x * BLOCK_ROWS, BLOCK_ROWS), BLOCK_ROWS)
    total[mine, :] = total[mine, :] + residual[...].astype(f32)
    for n in range(4):
        rows = total[n * BLOCK_ROWS : (n + 1) * BLOCK_ROWS, :].astype(bf16)
        picked = dot(sel[n].astype(bf16), rows, ((0,), (0,)))
        for q in range(4):
            lines[pl.ds(n * 4 + q, DEVICES, stride=16), :] = picked[:, q * 128 : (q + 1) * 128]
    sent[...] = lines[...].astype(bf16)


def logits_kernel(got, gain, mask, pick, place, vocab, sent, lines, lhs):
    square = jnp.zeros((8, 128), f32)
    logits = jnp.zeros((16, SHARD), f32)
    for b in range(BATCH):
        for c in range(2):
            value = jnp.zeros((16, 128), f32)
            for x in range(4):
                start = ((b * 4 + x) * 2 + c) * 16
                value = value + got[start : start + 16, :].astype(f32)
            lines[(b * 2 + c) * 16 : (b * 2 + c + 1) * 16, :] = value.astype(bf16).astype(f32)
        for q in range(4):
            n = b * 4 + q
            value = lines[pl.ds(b * 32 + q, 8, stride=4), :]
            square = square + value * value
            value = value * gain[n : n + 1, :]
            lhs[:, n * 128 : (n + 1) * 128] = jnp.concatenate([value, jnp.zeros_like(value)], 0).astype(bf16)
        part = slice(b * COLS, (b + 1) * COLS)
        logits = logits + dot(lhs[:, part], vocab[:, part], ((1,), (1,)))
    logits = logits[:8] * lax.rsqrt(jnp.sum(square, axis=1, keepdims=True) / D + epsilon)
    allowed = jnp.where(mask[...] > 0.5, jnp.exp(jnp.where(mask[...] > 0.5, logits, 0.0)), 0.0)
    totals = jnp.sum(allowed, axis=1, keepdims=True)
    picked = jnp.sum(jnp.where(pick[...] > 0.5, logits, 0.0), axis=1, keepdims=True)
    lane = iota((8, 128), 1)
    value = jnp.zeros((8, 128), f32)
    for n, (left, right) in enumerate(zip(split(totals, 3), split(picked, 3))):
        pair = jnp.where(lane % 4 < 2, left.astype(f32), right.astype(f32))
        value = jnp.where(lane // 4 == n, pair, value)
    sub = iota((8, 128), 0)
    for d in range(DEVICES):
        b, t = d // TENSOR, d % TENSOR
        i = d // 16
        row = b * 32 + ((t % 2) * 4 + t // 2) * 4
        j = (i % 2) * 4 + i // 2
        features = lines[row : row + 8, :]
        note = place[d : d + 1, :] * value[j : j + 1, :]
        group = jnp.where(sub < 4, features, jnp.where(sub == 4, note, 0.0))
        if d % 2 == 0:
            first = group
        else:
            sent[(d - 1) * 8 : (d + 1) * 8, :] = jnp.concatenate([first, group], 0).astype(bf16)


def finish_kernel(got, home, layer_out, token):
    found = dot(home[...], got[...])
    for q in range(4):
        layer_out[:, q * 128 : (q + 1) * 128] = found[q * BLOCK_ROWS : (q + 1) * BLOCK_ROWS].astype(bf16)
    sums = found[DEVICES : DEVICES + 1, :]
    totals = sums[:, 0:2] + sums[:, 4:6] + sums[:, 8:10]
    picked = sums[:, 2:4] + sums[:, 6:8] + sums[:, 10:12]
    token[...] = picked - jnp.log(totals)


def struct(shape, dtype):
    return jax.ShapeDtypeStruct(shape, dtype)


def far(*arrays):
    return [pltpu.with_memory_space_constraint(array, pltpu.HBM) for array in arrays]


def near(array):
    return pltpu.with_memory_space_constraint(array, pltpu.VMEM)


def params(mib):
    return pltpu.CompilerParams(vmem_limit_bytes=mib * 1024 * 1024)


def body(
    x_new,
    z_gate,
    bc_new,
    dt_raw,
    conv_x,
    conv_bc,
    conv_x_weight,
    conv_bc_weight,
    dt_bias,
    a_log,
    d_skip,
    ssm_state,
    norm_gain,
    out_weight,
    residual,
    final_gain,
    vocab_weight,
    tile_ids,
    tile_valid,
    sampled,
):
    tab = jnp.concatenate([tile_ids, tile_valid, sampled[:, None]], axis=1)
    sel, mask, pick, place, home = pl.pallas_call(
        tables_kernel,
        out_shape=(
            struct((4, BLOCK_ROWS, DEVICES), f32),
            struct((8, SHARD), f32),
            struct((8, SHARD), f32),
            struct((DEVICES, 128), f32),
            struct((DEVICES + 16, DEVICES * 8), bf16),
        ),
        in_specs=[VMEM],
        out_specs=(VMEM,) * 5,
        compiler_params=params(8),
        name="tables",
    )(tab)
    small = lambda *shape: pltpu.VMEM(shape, f32)
    half = lambda *shape: pltpu.VMEM(shape, bf16)
    state = ssm_state.reshape(ROWS, CHAN, STATE)
    sent, sx_t, b_pieces, decay = pl.pallas_call(
        ssm_kernel,
        out_shape=(
            struct((BATCH, LINES + 8, 128), bf16),
            struct((CHAN, 3 * ROWS), bf16),
            struct((3 * ROWS, STATE), f32),
            struct((ROWS, HEADS), f32),
        ),
        in_specs=[HBM] * 14,
        out_specs=(VMEM,) * 4,
        scratch_shapes=[
            half(ROWS, CHAN), half(ROWS, CHAN), half(ROWS, STATE), half(ROWS, STATE), small(ROWS, HEADS),
            half(3, ROWS, CHAN), half(3, ROWS, STATE), half(3, ROWS, STATE),
            small(4, CHAN), small(4, STATE), small(4, STATE),
            small(1, HEADS), small(1, HEADS), small(1, HEADS), small(1, CHAN), small(4, 128),
            half(ROWS, CHAN, STATE), small(CHAN, 128), half(STATE, 128), small(ROWS, STATE),
            pltpu.SemaphoreType.DMA((16,)), pltpu.SemaphoreType.DMA((ROWS // STEP,)),
        ],
        compiler_params=params(24),
        name="ssm",
    )(
        *far(x_new, z_gate, bc_new, dt_raw, jnp.swapaxes(conv_x, 0, 1), jnp.swapaxes(conv_bc, 0, 1),
        conv_x_weight, conv_bc_weight, dt_bias[None, :], a_log[None, :], d_skip[None, :], state,
        norm_gain[None, :], final_gain.reshape(4, 128))
    )
    new_state, state_done = pl.pallas_call(
        state_kernel,
        out_shape=(struct((ROWS, CHAN, STATE), bf16), struct((8, 128), f32)),
        in_specs=[HBM] + [VMEM] * 3,
        out_specs=(HBM, VMEM),
        scratch_shapes=[
            half(ROWS, CHAN, STATE),
            half(ROWS, CHAN, STATE),
            pltpu.SemaphoreType.DMA((ROWS // GROUP_ROWS,)),
            pltpu.SemaphoreType.DMA((ROWS // GROUP_ROWS,)),
        ],
        compiler_params=params(24),
        cost_estimate=pl.CostEstimate(flops=10**9, bytes_accessed=2 * ROWS * CHAN * STATE * 2, transcendentals=0),
        name="state",
    )(*far(state), sx_t, b_pieces, decay)
    got = lax.all_to_all(sent, "batch", 0, 0, tiled=True)
    sent, kept, gain_all = pl.pallas_call(
        project_kernel,
        out_shape=(
            struct((128, COLS + 128), bf16),
            struct((128, COLS + 128), f32),
            struct((BATCH * 4, 128), f32),
        ),
        in_specs=[VMEM] * 3 + [ANY] * 2,
        out_specs=(VMEM,) * 3,
        scratch_shapes=[half(BATCH * ROWS, CHAN)],
        compiler_params=params(16),
        cost_estimate=pl.CostEstimate(flops=5 * 10**9, bytes_accessed=10**7, transcendentals=0),
        name="project",
    )(got, out_weight, norm_gain[None, :], sel, state_done)
    got = lax.ppermute(sent, "tensor", [(t, t ^ 1) for t in range(TENSOR)])
    sent = pl.pallas_call(
        merge_kernel,
        out_shape=struct((DEVICES * 16, 128), bf16),
        in_specs=[VMEM] * 4,
        out_specs=VMEM,
        scratch_shapes=[small(128, COLS), small(DEVICES * 16, 128)],
        compiler_params=params(8),
        cost_estimate=pl.CostEstimate(flops=5 * 10**9, bytes_accessed=10**7, transcendentals=0),
        name="merge",
    )(got, kept, residual, sel)
    got = lax.all_to_all(sent.reshape(DEVICES, 16, 128), ("batch", "tensor"), 0, 0, tiled=True)
    sent = pl.pallas_call(
        logits_kernel,
        out_shape=struct((DEVICES * 8, 128), bf16),
        in_specs=[VMEM] * 6,
        out_specs=VMEM,
        scratch_shapes=[
            small(DEVICES * 4 + 8, 128),
            half(16, D),
        ],
        compiler_params=params(16),
        name="logits",
    )(got.reshape(DEVICES * 16, 128), gain_all, mask, pick, place, near(vocab_weight))
    got = lax.all_to_all(sent.reshape(DEVICES, 8, 128), ("batch", "tensor"), 0, 0, tiled=True)
    layer_out, token_logprob = pl.pallas_call(
        finish_kernel,
        out_shape=(struct((BLOCK_ROWS, COLS), bf16), struct((1, 2), f32)),
        in_specs=[VMEM] * 2,
        out_specs=(VMEM,) * 2,
        compiler_params=params(4),
        name="finish",
    )(got.reshape(DEVICES * 8, 128), home)
    token_logprob = token_logprob.reshape(2)
    return (new_state.reshape(ROWS, HEADS, HEAD_DIM, STATE), layer_out, token_logprob)


def solution(mesh):
    return jax.shard_map(
        body,
        mesh=mesh,
        in_specs=(
            P("batch", "tensor"),
            P("batch", "tensor"),
            P("batch", None),
            P("batch", "tensor"),
            P("batch", None, "tensor"),
            P("batch", None, None),
            P(None, "tensor"),
            P(),
            P("tensor"),
            P("tensor"),
            P("tensor"),
            P("batch", "tensor", None, None),
            P("tensor"),
            P("tensor", "batch"),
            P("tensor", "batch"),
            P("batch"),
            P(("batch", "tensor"), None),
            P(),
            P(),
            P(),
        ),
        out_specs=(P("batch", "tensor", None, None), P("tensor", "batch"), P(("batch", "tensor"))),
        check_vma=False,
    )
```

```python
import functools

import jax
import jax.numpy as jnp
from jax import lax
from jax.experimental import pallas as pl
from jax.experimental.pallas import tpu as pltpu
from jax.sharding import PartitionSpec as P

D = 8192
HEAD_DIM = 64
STATE = 256
GROUP_HEADS = 32
GROUPS = 4
TILE = 128
TILES_DEV = 4
BLOCK_ROWS = 32

ROWS = 16
CHAN = 1024
HEADS = 16
KB = CHAN // 128
LINES = KB * ROWS
COLS = 512
BATCH = 16
TENSOR = 8
DEVICES = BATCH * TENSOR
SHARD = TILES_DEV * TILE
STEP = 4
GROUP_ROWS = 4

epsilon = 1e-05
f32 = jnp.float32
bf16 = jnp.bfloat16
HBM = pl.BlockSpec(memory_space=pltpu.HBM)
ANY = pl.BlockSpec(memory_space=pl.ANY)
VMEM = pl.BlockSpec(memory_space=pltpu.VMEM)
HIGHEST = lax.Precision.HIGHEST


def split(value, parts):
    pieces = []
    for _ in range(parts):
        piece = value.astype(bf16)
        pieces.append(piece)
        value = value - piece.astype(f32)
    return pieces


def silu(value):
    return value / (1.0 + jnp.exp(-value))


def dot(a, b, contract=((1,), (0,)), precision=None):
    return lax.dot_general(a, b, (contract, ((), ())), precision=precision, preferred_element_type=f32)


def iota(shape, dim):
    return lax.broadcasted_iota(jnp.int32, shape, dim)


def tables_kernel(tab, sel, mask, pick, place, home):
    tensor = lax.axis_index("tensor")
    shard = lax.axis_index("batch") * TENSOR + tensor
    lanes = iota((BLOCK_ROWS, DEVICES), 1)
    for n in range(4):
        block = (2 * n + tensor % 2) * BLOCK_ROWS
        own = tab[pl.ds(pl.multiple_of(block, BLOCK_ROWS), BLOCK_ROWS), :]
        used = jnp.zeros((BLOCK_ROWS, DEVICES), f32)
        for slot in range(4):
            tiles = own[:, slot : slot + 1]
            valid = own[:, 4 + slot : 5 + slot]
            hit = jnp.where(valid == 1, tiles >> 2, -1) == lanes
            used = jnp.where(hit, 1.0, used)
        sel[n] = used
    rows = DEVICES * 2
    whole = tab[...]
    tile = shard * TILES_DEV + iota((rows, SHARD), 1) // TILE
    held = jnp.zeros((rows, SHARD), f32)
    mine = jnp.zeros((rows, 1), f32)
    for slot in range(4):
        tiles = jnp.where(whole[:, 4 + slot : 5 + slot] == 1, whole[:, slot : slot + 1], -1)
        held = jnp.where(tiles == tile, 1.0, held)
        mine = jnp.where((tiles >> 2) == shard, 1.0, mine)
    chosen = jnp.where(whole[:, 8:9] == shard * SHARD + iota((rows, SHARD), 1), 1.0, 0.0)
    order = iota((8, rows), 0)
    order = 2 * (order % 4) + order // 4
    block = jnp.where(iota((8, rows), 1) // BLOCK_ROWS == order, 1.0, 0.0).astype(bf16)
    mask[...] = dot(block, held.astype(bf16))
    pick[...] = dot(block, chosen.astype(bf16))
    lane = iota((rows, 128), 1)
    parity = (lane % 2 == iota((rows, 128), 0) % 2) & (lane < 12)
    spread = jnp.where(parity, mine, 0.0).astype(bf16)
    pairs = jnp.where(iota((DEVICES, rows), 1) // 2 == iota((DEVICES, rows), 0), 1.0, 0.0).astype(bf16)
    place[...] = dot(pairs, spread)
    own = tab[pl.ds(pl.multiple_of(tensor * BLOCK_ROWS, BLOCK_ROWS), BLOCK_ROWS), :]
    line = iota((BLOCK_ROWS, DEVICES * 8), 1)
    for q in range(4):
        found = line == (own[:, 8:9] // SHARD) * 8 + q
        home[q * BLOCK_ROWS : (q + 1) * BLOCK_ROWS, :] = jnp.where(found, 1.0, 0.0).astype(bf16)
    line = iota((16, DEVICES * 8), 1)
    found = (line % 8 == 4) & (iota((16, DEVICES * 8), 0) == 0)
    home[DEVICES : DEVICES + 16, :] = jnp.where(found, 1.0, 0.0).astype(bf16)


def ssm_kernel(
    x_new, z_gate, bc_new, dt_raw, conv_x, conv_bc, wx, wbc, dt_bias, a_log, d_skip, state, gain, final_gain, weight,
    sent, sx_t, b_pieces, decay_out, weight_near,
    x_v, z_v, b_v, c_v, dt_v, cx_v, cb_v, cc_v, wx_v, wb_v, wc_v, bias_v, alog_v, skip_v, gain_v, fg_v,
    state_v, acc, c_t, c_f, small_sem, in_sem, weight_sem,
):
    group = lax.axis_index("tensor") // 2
    first = pl.ds(pl.multiple_of(group * STATE, STATE), STATE)
    second = pl.ds(pl.multiple_of((GROUPS + group) * STATE, STATE), STATE)
    pairs = [
        (bc_new.at[:, second], c_v), (conv_bc.at[:, :, second], cc_v), (wbc.at[:, second], wc_v),
        (dt_raw, dt_v), (dt_bias, bias_v), (a_log, alog_v), (d_skip, skip_v),
        (conv_x, cx_v), (x_new, x_v), (wx, wx_v),
        (bc_new.at[:, first], b_v), (conv_bc.at[:, :, first], cb_v), (wbc.at[:, first], wb_v),
        (z_gate, z_v), (gain, gain_v), (final_gain, fg_v),
    ]
    copies = [pltpu.make_async_copy(src, dst, small_sem.at[n]) for n, (src, dst) in enumerate(pairs)]
    for copy in copies:
        copy.start()

    def rows_in(n):
        part = pl.ds(n * STEP, STEP)
        return pltpu.make_async_copy(state.at[part], state_v.at[part], in_sem.at[n])

    for n in range(ROWS // STEP):
        rows_in(n).start()
    weight_copy = pltpu.make_async_copy(weight, weight_near, weight_sem)
    weight_copy.start()

    def conv(window, newest, weight):
        total = newest[...].astype(f32) * weight[3:4, :]
        for k in range(3):
            total = total + window[k].astype(f32) * weight[k : k + 1, :]
        return silu(total)

    for copy in copies[:3]:
        copy.wait()
    c_out = conv(cc_v, c_v, wc_v)
    pieces = [piece.astype(f32) for piece in split(c_out, 3)]
    c_t[...] = jnp.concatenate(pieces + [jnp.zeros((128 - 3 * ROWS, STATE), f32)], 0).T.astype(bf16)
    acc[...] = jnp.zeros_like(acc)
    c_f[...] = c_out
    lane = iota((128, 128), 1)
    column = lane % ROWS

    def some_rows(n, carry):
        rows_in(n).wait()
        for m in range(CHAN // 128):
            part = slice(m * 128, (m + 1) * 128)
            total = acc[part, :]
            for k in range(STEP):
                r = n * STEP + k
                if k < 2:
                    total = jnp.where(column == r, dot(state_v[r, part, :], c_t[...]), total)
                else:
                    weighed = state_v[r, part, :].astype(f32) * c_f[pl.ds(r, 1), :]
                    total = jnp.where(lane == r, jnp.sum(weighed, axis=1, keepdims=True), total)
            acc[part, :] = total
        return carry

    lax.fori_loop(0, 3, some_rows, 0)
    for copy in copies[3:]:
        copy.wait()
    raw = dt_v[...] + bias_v[...]
    step = jnp.maximum(raw, 0.0) + jnp.log1p(jnp.exp(-jnp.abs(raw)))
    decay = jnp.exp(-jnp.exp(alog_v[...]) * step)
    decay_out[...] = decay
    spread = jnp.where(iota((HEADS, CHAN), 1) // HEAD_DIM == iota((HEADS, CHAN), 0), 1.0, 0.0)
    wide = dot(jnp.concatenate([step, decay, jnp.broadcast_to(skip_v[...], (8, HEADS))], 0), spread, precision=HIGHEST)
    step_c, decay_c, skip_c = wide[:ROWS], wide[ROWS : 2 * ROWS], wide[2 * ROWS : 2 * ROWS + 1]
    conv_out = conv(cx_v, x_v, wx_v)
    b_in = conv(cb_v, b_v, wb_v)
    sx = step_c * conv_out
    sx_hi, sx_lo = split(sx, 2)
    sx_t[...] = jnp.concatenate([sx_hi.astype(f32), sx_lo.astype(f32), sx_hi.astype(f32)], 0).T.astype(bf16)
    b_hi, b_lo = split(b_in, 2)
    b_pieces[...] = jnp.concatenate([b_hi.astype(f32), b_hi.astype(f32), b_lo.astype(f32)], 0)
    gate = silu(z_v[...].astype(f32)) * gain_v[...]
    lax.fori_loop(3, ROWS // STEP, some_rows, 0)
    inner = jnp.sum(b_in * c_out, axis=1, keepdims=True)
    total = acc[...].T
    total = total[:ROWS] + total[ROWS : 2 * ROWS] + total[2 * ROWS : 3 * ROWS]
    ssm_out = decay_c * total + sx * inner + skip_c * conv_out
    scaled = (ssm_out * gate).astype(bf16)
    hi, mid = [piece.astype(f32) for piece in split(fg_v[...], 2)]
    tail = jnp.concatenate([hi, mid], 0).astype(bf16)
    for b in range(BATCH):
        for k in range(KB):
            sent[b, k * ROWS : (k + 1) * ROWS, :] = scaled[:, k * 128 : (k + 1) * 128]
        sent[b, LINES : LINES + 8, :] = tail
    weight_copy.wait()


def state_kernel(state, sx_t, b_pieces, decay, new_state, done, state_v, out_v, in_sem, out_sem):
    done[...] = jnp.zeros_like(done)

    def rows_in(n):
        part = pl.ds(n * GROUP_ROWS, GROUP_ROWS)
        return pltpu.make_async_copy(state.at[part], state_v.at[part], in_sem.at[n])

    def rows_out(n):
        part = pl.ds(n * GROUP_ROWS, GROUP_ROWS)
        return pltpu.make_async_copy(out_v.at[part], new_state.at[part], out_sem.at[n])

    steps = ROWS // GROUP_ROWS
    for n in range(steps):
        rows_in(n).start()

    def some_rows(n, carry):
        rows_in(n).wait()
        for k in range(GROUP_ROWS):
            r = n * GROUP_ROWS + k
            on_row = iota((3 * ROWS, STATE), 0) % ROWS == r
            b_row = jnp.where(on_row, b_pieces[...], 0.0).astype(bf16)
            scale = decay[pl.ds(r, 1), :]
            for m in range(CHAN // 128):
                outer = dot(sx_t[m * 128 : (m + 1) * 128, :], b_row)
                for half in range(2):
                    head = 2 * m + half
                    rows = slice(head * HEAD_DIM, (head + 1) * HEAD_DIM)
                    fresh = scale[:, head : head + 1] * state_v[r, rows, :].astype(f32)
                    out_v[r, rows, :] = (fresh + outer[half * HEAD_DIM : (half + 1) * HEAD_DIM]).astype(bf16)
        rows_out(n).start()
        return carry

    lax.fori_loop(0, steps, some_rows, 0)

    def finish(n, carry):
        rows_out(n).wait()
        return carry

    lax.fori_loop(0, steps, finish, 0)


def project_kernel(got, weight, gain, tables_done, state_done, sent, kept, final_gain, lhs):
    core = lax.axis_index("tensor") % 2
    for side in range(2):
        parity = core if side else 1 - core
        for n in range(4):
            for e in range(2):
                b = 4 * n + 2 * parity + e
                to = (side * 8 + n * 2 + e) * ROWS
                for k in range(KB):
                    lhs[to : to + ROWS, k * 128 : (k + 1) * 128] = got[b, k * ROWS : (k + 1) * ROWS, :]
    for b in range(BATCH):
        pieces = got[b, LINES : LINES + 8, :].astype(f32)
        final_gain[b * 4 : b * 4 + 4, :] = pieces[0:4] + pieces[4:8]
    inverse = 1.0 / gain[...]
    inverse = inverse * inverse
    lane = iota((128, 128), 1)
    for side, out in enumerate((sent, kept)):
        rows = lhs[side * 128 : (side + 1) * 128, :]
        product = dot(rows, weight[...])
        wide = rows.astype(f32)
        square = jnp.sum(wide * wide * inverse, axis=1, keepdims=True)
        hi, mid, lo = [piece.astype(f32) for piece in split(square, 3)]
        tail = jnp.where(lane == 0, hi, jnp.where(lane == 1, mid, jnp.where(lane == 2, lo, 0.0)))
        out[:, :COLS] = product.astype(out.dtype)
        out[:, COLS:] = tail.astype(out.dtype)


def merge_kernel(got, kept, residual, sel, sent, total, lines):
    x = lax.axis_index("tensor") // 2
    both = got[...].astype(f32) + kept[...]
    square = jnp.sum(both[:, COLS:], axis=1, keepdims=True)
    total[...] = both[:, :COLS] * lax.rsqrt(square / (GROUP_HEADS * HEAD_DIM) + epsilon)
    mine = pl.ds(pl.multiple_of(x * BLOCK_ROWS, BLOCK_ROWS), BLOCK_ROWS)
    total[mine, :] = total[mine, :] + residual[...].astype(f32)
    for n in range(4):
        rows = total[n * BLOCK_ROWS : (n + 1) * BLOCK_ROWS, :].astype(bf16)
        picked = dot(sel[n].astype(bf16), rows, ((0,), (0,)))
        for q in range(4):
            lines[pl.ds(n * 4 + q, DEVICES, stride=16), :] = picked[:, q * 128 : (q + 1) * 128]
    sent[...] = lines[...].astype(bf16)


def logits_kernel(got, gain, mask, pick, place, vocab, sent, lines, lhs):
    square = jnp.zeros((8, 128), f32)
    logits = jnp.zeros((16, SHARD), f32)
    for b in range(BATCH):
        for c in range(2):
            value = jnp.zeros((16, 128), f32)
            for x in range(4):
                start = ((b * 4 + x) * 2 + c) * 16
                value = value + got[start : start + 16, :].astype(f32)
            lines[(b * 2 + c) * 16 : (b * 2 + c + 1) * 16, :] = value.astype(bf16).astype(f32)
        for q in range(4):
            n = b * 4 + q
            value = lines[pl.ds(b * 32 + q, 8, stride=4), :]
            square = square + value * value
            value = value * gain[n : n + 1, :]
            lhs[:, n * 128 : (n + 1) * 128] = jnp.concatenate([value, jnp.zeros_like(value)], 0).astype(bf16)
        part = slice(b * COLS, (b + 1) * COLS)
        logits = logits + dot(lhs[:, part], vocab[:, part], ((1,), (1,)))
    logits = logits[:8] * lax.rsqrt(jnp.sum(square, axis=1, keepdims=True) / D + epsilon)
    allowed = jnp.where(mask[...] > 0.5, jnp.exp(jnp.where(mask[...] > 0.5, logits, 0.0)), 0.0)
    totals = jnp.sum(allowed, axis=1, keepdims=True)
    picked = jnp.sum(jnp.where(pick[...] > 0.5, logits, 0.0), axis=1, keepdims=True)
    lane = iota((8, 128), 1)
    value = jnp.zeros((8, 128), f32)
    for n, (left, right) in enumerate(zip(split(totals, 3), split(picked, 3))):
        pair = jnp.where(lane % 4 < 2, left.astype(f32), right.astype(f32))
        value = jnp.where(lane // 4 == n, pair, value)
    sub = iota((8, 128), 0)
    for d in range(DEVICES):
        b, t = d // TENSOR, d % TENSOR
        i = d // 16
        row = b * 32 + ((t % 2) * 4 + t // 2) * 4
        j = (i % 2) * 4 + i // 2
        features = lines[row : row + 8, :]
        note = place[d : d + 1, :] * value[j : j + 1, :]
        group = jnp.where(sub < 4, features, jnp.where(sub == 4, note, 0.0))
        if d % 2 == 0:
            first = group
        else:
            sent[(d - 1) * 8 : (d + 1) * 8, :] = jnp.concatenate([first, group], 0).astype(bf16)


def finish_kernel(got, home, layer_out, token):
    found = dot(home[...], got[...])
    for q in range(4):
        layer_out[:, q * 128 : (q + 1) * 128] = found[q * BLOCK_ROWS : (q + 1) * BLOCK_ROWS].astype(bf16)
    sums = found[DEVICES : DEVICES + 1, :]
    totals = sums[:, 0:2] + sums[:, 4:6] + sums[:, 8:10]
    picked = sums[:, 2:4] + sums[:, 6:8] + sums[:, 10:12]
    token[...] = picked - jnp.log(totals)


def struct(shape, dtype):
    return jax.ShapeDtypeStruct(shape, dtype)


def far(*arrays):
    return [pltpu.with_memory_space_constraint(array, pltpu.HBM) for array in arrays]


def near(array):
    return pltpu.with_memory_space_constraint(array, pltpu.VMEM)


def params(mib):
    return pltpu.CompilerParams(vmem_limit_bytes=mib * 1024 * 1024)


def body(
    x_new,
    z_gate,
    bc_new,
    dt_raw,
    conv_x,
    conv_bc,
    conv_x_weight,
    conv_bc_weight,
    dt_bias,
    a_log,
    d_skip,
    ssm_state,
    norm_gain,
    out_weight,
    residual,
    final_gain,
    vocab_weight,
    tile_ids,
    tile_valid,
    sampled,
):
    tab = jnp.concatenate([tile_ids, tile_valid, sampled[:, None]], axis=1)
    sel, mask, pick, place, home = pl.pallas_call(
        tables_kernel,
        out_shape=(
            struct((4, BLOCK_ROWS, DEVICES), f32),
            struct((8, SHARD), f32),
            struct((8, SHARD), f32),
            struct((DEVICES, 128), f32),
            struct((DEVICES + 16, DEVICES * 8), bf16),
        ),
        in_specs=[VMEM],
        out_specs=(VMEM,) * 5,
        compiler_params=params(8),
        name="tables",
    )(tab)
    small = lambda *shape: pltpu.VMEM(shape, f32)
    half = lambda *shape: pltpu.VMEM(shape, bf16)
    state = ssm_state.reshape(ROWS, CHAN, STATE)
    sent, sx_t, b_pieces, decay, weight = pl.pallas_call(
        ssm_kernel,
        out_shape=(
            struct((BATCH, LINES + 8, 128), bf16),
            struct((CHAN, 3 * ROWS), bf16),
            struct((3 * ROWS, STATE), f32),
            struct((ROWS, HEADS), f32),
            struct((CHAN, COLS), bf16),
        ),
        in_specs=[HBM] * 15,
        out_specs=(VMEM,) * 5,
        scratch_shapes=[
            half(ROWS, CHAN), half(ROWS, CHAN), half(ROWS, STATE), half(ROWS, STATE), small(ROWS, HEADS),
            half(3, ROWS, CHAN), half(3, ROWS, STATE), half(3, ROWS, STATE),
            small(4, CHAN), small(4, STATE), small(4, STATE),
            small(1, HEADS), small(1, HEADS), small(1, HEADS), small(1, CHAN), small(4, 128),
            half(ROWS, CHAN, STATE), small(CHAN, 128), half(STATE, 128), small(ROWS, STATE),
            pltpu.SemaphoreType.DMA((16,)), pltpu.SemaphoreType.DMA((ROWS // STEP,)),
            pltpu.SemaphoreType.DMA,
        ],
        compiler_params=params(24),
        name="ssm",
    )(
        *far(x_new, z_gate, bc_new, dt_raw, jnp.swapaxes(conv_x, 0, 1), jnp.swapaxes(conv_bc, 0, 1),
        conv_x_weight, conv_bc_weight, dt_bias[None, :], a_log[None, :], d_skip[None, :], state,
        norm_gain[None, :], final_gain.reshape(4, 128), out_weight)
    )
    new_state, state_done = pl.pallas_call(
        state_kernel,
        out_shape=(struct((ROWS, CHAN, STATE), bf16), struct((8, 128), f32)),
        in_specs=[HBM] + [VMEM] * 3,
        out_specs=(HBM, VMEM),
        scratch_shapes=[
            half(ROWS, CHAN, STATE),
            half(ROWS, CHAN, STATE),
            pltpu.SemaphoreType.DMA((ROWS // GROUP_ROWS,)),
            pltpu.SemaphoreType.DMA((ROWS // GROUP_ROWS,)),
        ],
        compiler_params=params(24),
        cost_estimate=pl.CostEstimate(flops=10**9, bytes_accessed=2 * ROWS * CHAN * STATE * 2, transcendentals=0),
        name="state",
    )(*far(state), sx_t, b_pieces, decay)
    got = lax.all_to_all(sent, "batch", 0, 0, tiled=True)
    sent, kept, gain_all = pl.pallas_call(
        project_kernel,
        out_shape=(
            struct((128, COLS + 128), bf16),
            struct((128, COLS + 128), f32),
            struct((BATCH * 4, 128), f32),
        ),
        in_specs=[VMEM] * 3 + [ANY] * 2,
        out_specs=(VMEM,) * 3,
        scratch_shapes=[half(BATCH * ROWS, CHAN)],
        compiler_params=params(16),
        cost_estimate=pl.CostEstimate(flops=5 * 10**9, bytes_accessed=10**7, transcendentals=0),
        name="project",
    )(got, weight, norm_gain[None, :], sel, state_done)
    got = lax.ppermute(sent, "tensor", [(t, t ^ 1) for t in range(TENSOR)])
    sent = pl.pallas_call(
        merge_kernel,
        out_shape=struct((DEVICES * 16, 128), bf16),
        in_specs=[VMEM] * 4,
        out_specs=VMEM,
        scratch_shapes=[small(128, COLS), small(DEVICES * 16, 128)],
        compiler_params=params(8),
        cost_estimate=pl.CostEstimate(flops=5 * 10**9, bytes_accessed=10**7, transcendentals=0),
        name="merge",
    )(got, kept, residual, sel)
    got = lax.all_to_all(sent.reshape(DEVICES, 16, 128), ("batch", "tensor"), 0, 0, tiled=True)
    sent = pl.pallas_call(
        logits_kernel,
        out_shape=struct((DEVICES * 8, 128), bf16),
        in_specs=[VMEM] * 6,
        out_specs=VMEM,
        scratch_shapes=[
            small(DEVICES * 4 + 8, 128),
            half(16, D),
        ],
        compiler_params=params(16),
        name="logits",
    )(got.reshape(DEVICES * 16, 128), gain_all, mask, pick, place, near(vocab_weight))
    got = lax.all_to_all(sent.reshape(DEVICES, 8, 128), ("batch", "tensor"), 0, 0, tiled=True)
    layer_out, token_logprob = pl.pallas_call(
        finish_kernel,
        out_shape=(struct((BLOCK_ROWS, COLS), bf16), struct((1, 2), f32)),
        in_specs=[VMEM] * 2,
        out_specs=(VMEM,) * 2,
        compiler_params=params(4),
        name="finish",
    )(got.reshape(DEVICES * 8, 128), home)
    token_logprob = token_logprob.reshape(2)
    return (new_state.reshape(ROWS, HEADS, HEAD_DIM, STATE), layer_out, token_logprob)


def solution(mesh):
    return jax.shard_map(
        body,
        mesh=mesh,
        in_specs=(
            P("batch", "tensor"),
            P("batch", "tensor"),
            P("batch", None),
            P("batch", "tensor"),
            P("batch", None, "tensor"),
            P("batch", None, None),
            P(None, "tensor"),
            P(),
            P("tensor"),
            P("tensor"),
            P("tensor"),
            P("batch", "tensor", None, None),
            P("tensor"),
            P("tensor", "batch"),
            P("tensor", "batch"),
            P("batch"),
            P(("batch", "tensor"), None),
            P(),
            P(),
            P(),
        ),
        out_specs=(P("batch", "tensor", None, None), P("tensor", "batch"), P(("batch", "tensor"))),
        check_vma=False,
    )
```

```python
import functools

import jax
import jax.numpy as jnp
from jax import lax
from jax.experimental import pallas as pl
from jax.experimental.pallas import tpu as pltpu
from jax.sharding import PartitionSpec as P

D = 8192
HEAD_DIM = 64
STATE = 256
GROUP_HEADS = 32
GROUPS = 4
TILE = 128
TILES_DEV = 4
BLOCK_ROWS = 32

ROWS = 16
CHAN = 1024
HEADS = 16
KB = CHAN // 128
LINES = KB * ROWS
COLS = 512
BATCH = 16
TENSOR = 8
DEVICES = BATCH * TENSOR
SHARD = TILES_DEV * TILE
STEP = 4
GROUP_ROWS = 4

epsilon = 1e-05
f32 = jnp.float32
bf16 = jnp.bfloat16
HBM = pl.BlockSpec(memory_space=pltpu.HBM)
ANY = pl.BlockSpec(memory_space=pl.ANY)
VMEM = pl.BlockSpec(memory_space=pltpu.VMEM)
HIGHEST = lax.Precision.HIGHEST


def split(value, parts):
    pieces = []
    for _ in range(parts):
        piece = value.astype(bf16)
        pieces.append(piece)
        value = value - piece.astype(f32)
    return pieces


def silu(value):
    return value / (1.0 + jnp.exp(-value))


def dot(a, b, contract=((1,), (0,)), precision=None):
    return lax.dot_general(a, b, (contract, ((), ())), precision=precision, preferred_element_type=f32)


def iota(shape, dim):
    return lax.broadcasted_iota(jnp.int32, shape, dim)


def tables_kernel(tab, sel, mask, pick, place, home):
    tensor = lax.axis_index("tensor")
    shard = lax.axis_index("batch") * TENSOR + tensor
    lanes = iota((BLOCK_ROWS, DEVICES), 1)
    for n in range(4):
        block = (2 * n + tensor % 2) * BLOCK_ROWS
        own = tab[pl.ds(pl.multiple_of(block, BLOCK_ROWS), BLOCK_ROWS), :]
        used = jnp.zeros((BLOCK_ROWS, DEVICES), f32)
        for slot in range(4):
            tiles = own[:, slot : slot + 1]
            valid = own[:, 4 + slot : 5 + slot]
            hit = jnp.where(valid == 1, tiles >> 2, -1) == lanes
            used = jnp.where(hit, 1.0, used)
        sel[n] = used
    rows = DEVICES * 2
    whole = tab[...]
    tile = shard * TILES_DEV + iota((rows, SHARD), 1) // TILE
    held = jnp.zeros((rows, SHARD), f32)
    mine = jnp.zeros((rows, 1), f32)
    for slot in range(4):
        tiles = jnp.where(whole[:, 4 + slot : 5 + slot] == 1, whole[:, slot : slot + 1], -1)
        held = jnp.where(tiles == tile, 1.0, held)
        mine = jnp.where((tiles >> 2) == shard, 1.0, mine)
    chosen = jnp.where(whole[:, 8:9] == shard * SHARD + iota((rows, SHARD), 1), 1.0, 0.0)
    order = iota((8, rows), 0)
    order = 2 * (order % 4) + order // 4
    block = jnp.where(iota((8, rows), 1) // BLOCK_ROWS == order, 1.0, 0.0).astype(bf16)
    mask[...] = dot(block, held.astype(bf16))
    pick[...] = dot(block, chosen.astype(bf16))
    lane = iota((rows, 128), 1)
    parity = (lane % 2 == iota((rows, 128), 0) % 2) & (lane < 12)
    spread = jnp.where(parity, mine, 0.0).astype(bf16)
    pairs = jnp.where(iota((DEVICES, rows), 1) // 2 == iota((DEVICES, rows), 0), 1.0, 0.0).astype(bf16)
    place[...] = dot(pairs, spread)
    own = tab[pl.ds(pl.multiple_of(tensor * BLOCK_ROWS, BLOCK_ROWS), BLOCK_ROWS), :]
    line = iota((BLOCK_ROWS, DEVICES * 8), 1)
    for q in range(4):
        found = line == (own[:, 8:9] // SHARD) * 8 + q
        home[q * BLOCK_ROWS : (q + 1) * BLOCK_ROWS, :] = jnp.where(found, 1.0, 0.0).astype(bf16)
    line = iota((16, DEVICES * 8), 1)
    found = (line % 8 == 4) & (iota((16, DEVICES * 8), 0) == 0)
    home[DEVICES : DEVICES + 16, :] = jnp.where(found, 1.0, 0.0).astype(bf16)


def ssm_kernel(
    x_new, z_gate, bc_new, dt_raw, conv_x, conv_bc, wx, wbc, dt_bias, a_log, d_skip, state, gain, final_gain,
    sent, sx_t, b_pieces, decay_out,
    x_v, z_v, b_v, c_v, dt_v, cx_v, cb_v, cc_v, wx_v, wb_v, wc_v, bias_v, alog_v, skip_v, gain_v, fg_v,
    state_v, acc, c_t, c_f, small_sem, in_sem,
):
    group = lax.axis_index("tensor") // 2
    first = pl.ds(pl.multiple_of(group * STATE, STATE), STATE)
    second = pl.ds(pl.multiple_of((GROUPS + group) * STATE, STATE), STATE)
    pairs = [
        (bc_new.at[:, second], c_v), (conv_bc.at[:, :, second], cc_v), (wbc.at[:, second], wc_v),
        (dt_raw, dt_v), (dt_bias, bias_v), (a_log, alog_v), (d_skip, skip_v),
        (conv_x, cx_v), (x_new, x_v), (wx, wx_v),
        (bc_new.at[:, first], b_v), (conv_bc.at[:, :, first], cb_v), (wbc.at[:, first], wb_v),
        (z_gate, z_v), (gain, gain_v), (final_gain, fg_v),
    ]
    copies = [pltpu.make_async_copy(src, dst, small_sem.at[n]) for n, (src, dst) in enumerate(pairs)]
    for copy in copies:
        copy.start()

    def rows_in(n):
        part = pl.ds(n * STEP, STEP)
        return pltpu.make_async_copy(state.at[part], state_v.at[part], in_sem.at[n])

    for n in range(ROWS // STEP):
        rows_in(n).start()

    def conv(window, newest, weight):
        total = newest[...].astype(f32) * weight[3:4, :]
        for k in range(3):
            total = total + window[k].astype(f32) * weight[k : k + 1, :]
        return silu(total)

    for copy in copies[:3]:
        copy.wait()
    c_out = conv(cc_v, c_v, wc_v)
    pieces = [piece.astype(f32) for piece in split(c_out, 3)]
    c_t[...] = jnp.concatenate(pieces + [jnp.zeros((128 - 3 * ROWS, STATE), f32)], 0).T.astype(bf16)
    acc[...] = jnp.zeros_like(acc)
    c_f[...] = c_out
    lane = iota((128, 128), 1)
    column = lane % ROWS

    def some_rows(n, carry):
        rows_in(n).wait()
        for m in range(CHAN // 128):
            part = slice(m * 128, (m + 1) * 128)
            total = acc[part, :]
            for k in range(STEP):
                r = n * STEP + k
                if k < 2:
                    total = jnp.where(column == r, dot(state_v[r, part, :], c_t[...]), total)
                else:
                    weighed = state_v[r, part, :].astype(f32) * c_f[pl.ds(r, 1), :]
                    total = jnp.where(lane == r, jnp.sum(weighed, axis=1, keepdims=True), total)
            acc[part, :] = total
        return carry

    lax.fori_loop(0, 3, some_rows, 0)
    for copy in copies[3:]:
        copy.wait()
    raw = dt_v[...] + bias_v[...]
    step = jnp.maximum(raw, 0.0) + jnp.log1p(jnp.exp(-jnp.abs(raw)))
    decay = jnp.exp(-jnp.exp(alog_v[...]) * step)
    decay_out[...] = decay
    spread = jnp.where(iota((HEADS, CHAN), 1) // HEAD_DIM == iota((HEADS, CHAN), 0), 1.0, 0.0)
    wide = dot(jnp.concatenate([step, decay, jnp.broadcast_to(skip_v[...], (8, HEADS))], 0), spread, precision=HIGHEST)
    step_c, decay_c, skip_c = wide[:ROWS], wide[ROWS : 2 * ROWS], wide[2 * ROWS : 2 * ROWS + 1]
    conv_out = conv(cx_v, x_v, wx_v)
    b_in = conv(cb_v, b_v, wb_v)
    sx = step_c * conv_out
    sx_hi, sx_lo = split(sx, 2)
    sx_t[...] = jnp.concatenate([sx_hi.astype(f32), sx_lo.astype(f32), sx_hi.astype(f32)], 0).T.astype(bf16)
    b_hi, b_lo = split(b_in, 2)
    b_pieces[...] = jnp.concatenate([b_hi.astype(f32), b_hi.astype(f32), b_lo.astype(f32)], 0)
    gate = silu(z_v[...].astype(f32)) * gain_v[...]
    lax.fori_loop(3, ROWS // STEP, some_rows, 0)
    inner = jnp.sum(b_in * c_out, axis=1, keepdims=True)
    total = acc[...].T
    total = total[:ROWS] + total[ROWS : 2 * ROWS] + total[2 * ROWS : 3 * ROWS]
    ssm_out = decay_c * total + sx * inner + skip_c * conv_out
    scaled = (ssm_out * gate).astype(bf16)
    hi, mid = [piece.astype(f32) for piece in split(fg_v[...], 2)]
    tail = jnp.concatenate([hi, mid], 0).astype(bf16)
    for b in range(BATCH):
        for k in range(KB):
            sent[b, k * ROWS : (k + 1) * ROWS, :] = scaled[:, k * 128 : (k + 1) * 128]
        sent[b, LINES : LINES + 8, :] = tail


def state_kernel(state, sx_t, b_pieces, decay, new_state, done, state_v, out_v, in_sem, out_sem):
    done[...] = jnp.zeros_like(done)

    def rows_in(n):
        part = pl.ds(n * GROUP_ROWS, GROUP_ROWS)
        return pltpu.make_async_copy(state.at[part], state_v.at[part], in_sem.at[n])

    def rows_out(n):
        part = pl.ds(n * GROUP_ROWS, GROUP_ROWS)
        return pltpu.make_async_copy(out_v.at[part], new_state.at[part], out_sem.at[n])

    steps = ROWS // GROUP_ROWS
    for n in range(steps):
        rows_in(n).start()

    def some_rows(n, carry):
        rows_in(n).wait()
        for k in range(GROUP_ROWS):
            r = n * GROUP_ROWS + k
            on_row = iota((3 * ROWS, STATE), 0) % ROWS == r
            b_row = jnp.where(on_row, b_pieces[...], 0.0).astype(bf16)
            scale = decay[pl.ds(r, 1), :]
            for m in range(CHAN // 128):
                outer = dot(sx_t[m * 128 : (m + 1) * 128, :], b_row)
                for half in range(2):
                    head = 2 * m + half
                    rows = slice(head * HEAD_DIM, (head + 1) * HEAD_DIM)
                    fresh = scale[:, head : head + 1] * state_v[r, rows, :].astype(f32)
                    out_v[r, rows, :] = (fresh + outer[half * HEAD_DIM : (half + 1) * HEAD_DIM]).astype(bf16)
        rows_out(n).start()
        return carry

    lax.fori_loop(0, steps, some_rows, 0)

    def finish(n, carry):
        rows_out(n).wait()
        return carry

    lax.fori_loop(0, steps, finish, 0)


def project_kernel(got, weight, gain, tables_done, state_done, sent, kept, final_gain, lhs):
    core = lax.axis_index("tensor") % 2
    for side in range(2):
        parity = core if side else 1 - core
        for n in range(4):
            for e in range(2):
                b = 4 * n + 2 * parity + e
                to = (side * 8 + n * 2 + e) * ROWS
                for k in range(KB):
                    lhs[to : to + ROWS, k * 128 : (k + 1) * 128] = got[b, k * ROWS : (k + 1) * ROWS, :]
    for b in range(BATCH):
        pieces = got[b, LINES : LINES + 8, :].astype(f32)
        final_gain[b * 4 : b * 4 + 4, :] = pieces[0:4] + pieces[4:8]
    inverse = 1.0 / gain[...]
    inverse = inverse * inverse
    lane = iota((128, 128), 1)
    for side, out in enumerate((sent, kept)):
        rows = lhs[side * 128 : (side + 1) * 128, :]
        product = dot(rows, weight[...])
        wide = rows.astype(f32)
        square = jnp.sum(wide * wide * inverse, axis=1, keepdims=True)
        hi, mid, lo = [piece.astype(f32) for piece in split(square, 3)]
        tail = jnp.where(lane == 0, hi, jnp.where(lane == 1, mid, jnp.where(lane == 2, lo, 0.0)))
        out[:, :COLS] = product.astype(out.dtype)
        out[:, COLS:] = tail.astype(out.dtype)


def merge_kernel(got, kept, residual, sel, sent, total, lines):
    x = lax.axis_index("tensor") // 2
    both = got[...].astype(f32) + kept[...]
    square = jnp.sum(both[:, COLS:], axis=1, keepdims=True)
    total[...] = both[:, :COLS] * lax.rsqrt(square / (GROUP_HEADS * HEAD_DIM) + epsilon)
    mine = pl.ds(pl.multiple_of(x * BLOCK_ROWS, BLOCK_ROWS), BLOCK_ROWS)
    total[mine, :] = total[mine, :] + residual[...].astype(f32)
    for n in range(4):
        rows = total[n * BLOCK_ROWS : (n + 1) * BLOCK_ROWS, :].astype(bf16)
        picked = dot(sel[n].astype(bf16), rows, ((0,), (0,)))
        for q in range(4):
            lines[pl.ds(n * 4 + q, DEVICES, stride=16), :] = picked[:, q * 128 : (q + 1) * 128]
    sent[...] = lines[...].astype(bf16)


def logits_kernel(got, gain, mask, pick, place, vocab, sent, lines, lhs):
    square = jnp.zeros((8, 128), f32)
    logits = jnp.zeros((16, SHARD), f32)
    for b in range(BATCH):
        for c in range(2):
            value = jnp.zeros((16, 128), f32)
            for x in range(4):
                start = ((b * 4 + x) * 2 + c) * 16
                value = value + got[start : start + 16, :].astype(f32)
            lines[(b * 2 + c) * 16 : (b * 2 + c + 1) * 16, :] = value
        for q in range(4):
            n = b * 4 + q
            value = lines[pl.ds(b * 32 + q, 8, stride=4), :]
            square = square + value * value
            value = value * gain[n : n + 1, :]
            lhs[:, n * 128 : (n + 1) * 128] = jnp.concatenate([value, jnp.zeros_like(value)], 0).astype(bf16)
        part = slice(b * COLS, (b + 1) * COLS)
        logits = logits + dot(lhs[:, part], vocab[:, part], ((1,), (1,)))
    logits = logits[:8] * lax.rsqrt(jnp.sum(square, axis=1, keepdims=True) / D + epsilon)
    allowed = jnp.where(mask[...] > 0.5, jnp.exp(jnp.where(mask[...] > 0.5, logits, 0.0)), 0.0)
    totals = jnp.sum(allowed, axis=1, keepdims=True)
    picked = jnp.sum(jnp.where(pick[...] > 0.5, logits, 0.0), axis=1, keepdims=True)
    lane = iota((8, 128), 1)
    value = jnp.zeros((8, 128), f32)
    for n, (left, right) in enumerate(zip(split(totals, 3), split(picked, 3))):
        pair = jnp.where(lane % 4 < 2, left.astype(f32), right.astype(f32))
        value = jnp.where(lane // 4 == n, pair, value)
    sub = iota((8, 128), 0)
    for d in range(DEVICES):
        b, t = d // TENSOR, d % TENSOR
        i = d // 16
        row = b * 32 + ((t % 2) * 4 + t // 2) * 4
        j = (i % 2) * 4 + i // 2
        features = lines[row : row + 8, :]
        note = place[d : d + 1, :] * value[j : j + 1, :]
        group = jnp.where(sub < 4, features, jnp.where(sub == 4, note, 0.0))
        if d % 2 == 0:
            first = group
        else:
            sent[(d - 1) * 8 : (d + 1) * 8, :] = jnp.concatenate([first, group], 0).astype(bf16)


def finish_kernel(got, home, layer_out, token):
    found = dot(home[...], got[...])
    for q in range(4):
        layer_out[:, q * 128 : (q + 1) * 128] = found[q * BLOCK_ROWS : (q + 1) * BLOCK_ROWS].astype(bf16)
    sums = found[DEVICES : DEVICES + 1, :]
    totals = sums[:, 0:2] + sums[:, 4:6] + sums[:, 8:10]
    picked = sums[:, 2:4] + sums[:, 6:8] + sums[:, 10:12]
    token[...] = picked - jnp.log(totals)


def struct(shape, dtype):
    return jax.ShapeDtypeStruct(shape, dtype)


def far(*arrays):
    return [pltpu.with_memory_space_constraint(array, pltpu.HBM) for array in arrays]


def near(array):
    return pltpu.with_memory_space_constraint(array, pltpu.VMEM)


def params(mib):
    return pltpu.CompilerParams(vmem_limit_bytes=mib * 1024 * 1024)


def body(
    x_new,
    z_gate,
    bc_new,
    dt_raw,
    conv_x,
    conv_bc,
    conv_x_weight,
    conv_bc_weight,
    dt_bias,
    a_log,
    d_skip,
    ssm_state,
    norm_gain,
    out_weight,
    residual,
    final_gain,
    vocab_weight,
    tile_ids,
    tile_valid,
    sampled,
):
    tab = jnp.concatenate([tile_ids, tile_valid, sampled[:, None]], axis=1)
    sel, mask, pick, place, home = pl.pallas_call(
        tables_kernel,
        out_shape=(
            struct((4, BLOCK_ROWS, DEVICES), f32),
            struct((8, SHARD), f32),
            struct((8, SHARD), f32),
            struct((DEVICES, 128), f32),
            struct((DEVICES + 16, DEVICES * 8), bf16),
        ),
        in_specs=[VMEM],
        out_specs=(VMEM,) * 5,
        compiler_params=params(8),
        name="tables",
    )(tab)
    small = lambda *shape: pltpu.VMEM(shape, f32)
    half = lambda *shape: pltpu.VMEM(shape, bf16)
    state = ssm_state.reshape(ROWS, CHAN, STATE)
    sent, sx_t, b_pieces, decay = pl.pallas_call(
        ssm_kernel,
        out_shape=(
            struct((BATCH, LINES + 8, 128), bf16),
            struct((CHAN, 3 * ROWS), bf16),
            struct((3 * ROWS, STATE), f32),
            struct((ROWS, HEADS), f32),
        ),
        in_specs=[HBM] * 14,
        out_specs=(VMEM,) * 4,
        scratch_shapes=[
            half(ROWS, CHAN), half(ROWS, CHAN), half(ROWS, STATE), half(ROWS, STATE), small(ROWS, HEADS),
            half(3, ROWS, CHAN), half(3, ROWS, STATE), half(3, ROWS, STATE),
            small(4, CHAN), small(4, STATE), small(4, STATE),
            small(1, HEADS), small(1, HEADS), small(1, HEADS), small(1, CHAN), small(4, 128),
            half(ROWS, CHAN, STATE), small(CHAN, 128), half(STATE, 128), small(ROWS, STATE),
            pltpu.SemaphoreType.DMA((16,)), pltpu.SemaphoreType.DMA((ROWS // STEP,)),
        ],
        compiler_params=params(24),
        name="ssm",
    )(
        *far(x_new, z_gate, bc_new, dt_raw, jnp.swapaxes(conv_x, 0, 1), jnp.swapaxes(conv_bc, 0, 1),
        conv_x_weight, conv_bc_weight, dt_bias[None, :], a_log[None, :], d_skip[None, :], state,
        norm_gain[None, :], final_gain.reshape(4, 128))
    )
    new_state, state_done = pl.pallas_call(
        state_kernel,
        out_shape=(struct((ROWS, CHAN, STATE), bf16), struct((8, 128), f32)),
        in_specs=[HBM] + [VMEM] * 3,
        out_specs=(HBM, VMEM),
        scratch_shapes=[
            half(ROWS, CHAN, STATE),
            half(ROWS, CHAN, STATE),
            pltpu.SemaphoreType.DMA((ROWS // GROUP_ROWS,)),
            pltpu.SemaphoreType.DMA((ROWS // GROUP_ROWS,)),
        ],
        compiler_params=params(24),
        cost_estimate=pl.CostEstimate(flops=10**9, bytes_accessed=2 * ROWS * CHAN * STATE * 2, transcendentals=0),
        name="state",
    )(*far(state), sx_t, b_pieces, decay)
    got = lax.all_to_all(sent, "batch", 0, 0, tiled=True)
    sent, kept, gain_all = pl.pallas_call(
        project_kernel,
        out_shape=(
            struct((128, COLS + 128), bf16),
            struct((128, COLS + 128), f32),
            struct((BATCH * 4, 128), f32),
        ),
        in_specs=[VMEM] * 3 + [ANY] * 2,
        out_specs=(VMEM,) * 3,
        scratch_shapes=[half(BATCH * ROWS, CHAN)],
        compiler_params=params(16),
        cost_estimate=pl.CostEstimate(flops=5 * 10**9, bytes_accessed=10**7, transcendentals=0),
        name="project",
    )(got, out_weight, norm_gain[None, :], sel, state_done)
    got = lax.ppermute(sent, "tensor", [(t, t ^ 1) for t in range(TENSOR)])
    sent = pl.pallas_call(
        merge_kernel,
        out_shape=struct((DEVICES * 16, 128), bf16),
        in_specs=[VMEM] * 4,
        out_specs=VMEM,
        scratch_shapes=[small(128, COLS), small(DEVICES * 16, 128)],
        compiler_params=params(8),
        cost_estimate=pl.CostEstimate(flops=5 * 10**9, bytes_accessed=10**7, transcendentals=0),
        name="merge",
    )(got, kept, residual, sel)
    got = lax.all_to_all(sent.reshape(DEVICES, 16, 128), ("batch", "tensor"), 0, 0, tiled=True)
    sent = pl.pallas_call(
        logits_kernel,
        out_shape=struct((DEVICES * 8, 128), bf16),
        in_specs=[VMEM] * 6,
        out_specs=VMEM,
        scratch_shapes=[
            small(DEVICES * 4 + 8, 128),
            half(16, D),
        ],
        compiler_params=params(16),
        name="logits",
    )(got.reshape(DEVICES * 16, 128), gain_all, mask, pick, place, near(vocab_weight))
    got = lax.all_to_all(sent.reshape(DEVICES, 8, 128), ("batch", "tensor"), 0, 0, tiled=True)
    layer_out, token_logprob = pl.pallas_call(
        finish_kernel,
        out_shape=(struct((BLOCK_ROWS, COLS), bf16), struct((1, 2), f32)),
        in_specs=[VMEM] * 2,
        out_specs=(VMEM,) * 2,
        compiler_params=params(4),
        name="finish",
    )(got.reshape(DEVICES * 8, 128), home)
    token_logprob = token_logprob.reshape(2)
    return (new_state.reshape(ROWS, HEADS, HEAD_DIM, STATE), layer_out, token_logprob)


def solution(mesh):
    return jax.shard_map(
        body,
        mesh=mesh,
        in_specs=(
            P("batch", "tensor"),
            P("batch", "tensor"),
            P("batch", None),
            P("batch", "tensor"),
            P("batch", None, "tensor"),
            P("batch", None, None),
            P(None, "tensor"),
            P(),
            P("tensor"),
            P("tensor"),
            P("tensor"),
            P("batch", "tensor", None, None),
            P("tensor"),
            P("tensor", "batch"),
            P("tensor", "batch"),
            P("batch"),
            P(("batch", "tensor"), None),
            P(),
            P(),
            P(),
        ),
        out_specs=(P("batch", "tensor", None, None), P("tensor", "batch"), P(("batch", "tensor"))),
        check_vma=False,
    )
```
